256 devices in a mesh: section: 8 (over y, z_lo), dp: 32 (over z_hi, x, core).
Axes of the slice: x: 4, y: 4, z: 8 (z_hi: 4, z_lo: 2; z = z_hi * 2 + z_lo), core: 2. Of those that a mesh axis runs over, the one named last changes fastest.
Arguments:
- pre_norm: bfloat16 [2, 32, 48, 4096], P(None, 'dp'), may hold values from -12 to 12
- norm_gain: float32 [4096], replicated, may hold values from 0.3 to 3
- queries: bfloat16 [8, 2, 32, 128, 2048], P('section', None, 'dp'), may hold values from -24 to 24
- keys: bfloat16 [8, 2, 32, 48, 2048], P('section', None, 'dp'), may hold values from -6 to 6
- values: bfloat16 [8, 2, 32, 48, 2048], P('section', None, 'dp'), may hold values from -6 to 6
- head_grad: bfloat16 [8, 2, 32, 128, 2048], P('section', None, 'dp'), may hold values from -2 to 2
- key_weight: bfloat16 [8, 4096, 2048], P('section', 'dp'), may hold values from -0.09375 to 0.09375
- value_weight: bfloat16 [8, 4096, 2048], P('section', 'dp'), may hold values from -0.09375 to 0.09375
Outputs:
- query_grad: bfloat16 [8, 2, 32, 128, 2048], P('section', None, 'dp')
- key_weight_grad: bfloat16 [8, 4096, 2048], P('section', 'dp')
- value_weight_grad: bfloat16 [8, 4096, 2048], P('section', 'dp')
- encoder_grad: bfloat16 [2, 32, 48, 4096], P(None, 'dp')
- gain_grad: float32 [4096], replicated
The draws below stay inside these ranges and needn't reach their ends.
All inputs are finite; a program needn't handle non-finite values.
Results may differ from the reference program's by a relative error of at most 0.02.
Values may be sent and summed in bfloat16 or wider, within the bound.
No kernel may reach another device: no remote copies, remote signals or barrier semaphores. Data moves between devices by JAX's collectives and lax.ppermute only.
A program may use at most 128 MiB of HBM per device.

```python
import math
import jax
import jax.numpy as jnp
from jax import lax

D = 4096
HEAD_DIM = 64
MICRO = 2
TGT = 128
SRC = 48
HD = 2048
LAYERS = 8
SEQS = 32


def paired_keys(key):
    return jnp.clip(jax.random.normal(key, (LAYERS, MICRO, SEQS, SRC, HD), jnp.float32), -6.0, 6.0)


def draw_keys(key, part):
    base_keys = paired_keys(key)
    return base_keys.astype(jnp.bfloat16)


def draw_queries(key, part):
    key = jax.random.fold_in(key, 5)
    full_shape = (LAYERS, MICRO, SEQS, TGT, HD)
    result = 0.25 * jnp.clip(jax.random.normal(key, full_shape, jnp.float32), -6.0, 6.0)
    return result.astype(jnp.bfloat16)


def draw_pre_norm(key, part):
    key = jax.random.fold_in(key, 7)
    first_key, second_key, third_key = jax.random.split(key, 3)
    full_shape = (MICRO, SEQS, SRC, D)
    row_scale = jnp.exp(jax.random.uniform(first_key, (MICRO, SEQS, SRC, 1), jnp.float32, math.log(0.1), 0.0))
    col_scale = jnp.exp(jax.random.uniform(second_key, (D,), jnp.float32, math.log(0.3), math.log(3.0)))
    noise = jnp.clip(jax.random.normal(third_key, full_shape, jnp.float32), -4.0, 4.0)
    return (noise * row_scale * col_scale).astype(jnp.bfloat16)


def block_levels(rng, dims, shards, smallest, largest):
    factor_of = 1.0
    for dim, parts in shards:
        draws = jax.random.uniform(jax.random.fold_in(jax.random.fold_in(rng, 6), dim), (parts,), jnp.float32, smallest / len(shards), largest / len(shards))
        factor_of = factor_of * jnp.repeat(jnp.exp(draws), dims[dim] // parts).reshape((-1,) + (1,) * (len(dims) - 1 - dim))
    return factor_of


def gaussian(key, shape, scale, bound, cuts=(), dtype=jnp.bfloat16):
    entries = jax.random.normal(key, shape, jnp.float32) * scale
    if len(cuts) > 0:
        entries = block_levels(key, shape, cuts, -0.22, 0.18) * entries
    return jnp.clip(entries, min=-bound, max=bound).astype(dtype)


def setup_inputs(seed: int = 0) -> dict:
    splits = jax.random.split(jax.random.key(seed), 9)
    pre_norm = draw_pre_norm(jax.random.fold_in(splits[8], 71), 0)
    norm_gain = jnp.clip(jnp.exp(jax.random.uniform(splits[1], (D,), jnp.float32, math.log(0.3), math.log(3.0))), 0.3, 3.0)
    queries = draw_queries(jax.random.fold_in(splits[8], 71), 0)
    keys = draw_keys(jax.random.fold_in(splits[8], 71), 0)
    values = gaussian(splits[4], (LAYERS, MICRO, SEQS, SRC, HD), 1.0, 6.0, ((0, 8), (2, 32)))
    head_grad = gaussian(splits[5], (LAYERS, MICRO, SEQS, TGT, HD), 0.3, 2.0, ((0, 8), (2, 32)))
    key_weight = gaussian(splits[6], (LAYERS, D, HD), D ** -0.5, 0.09375, ((0, 8), (1, 32)))
    value_weight = gaussian(splits[7], (LAYERS, D, HD), D ** -0.5, 0.09375, ((0, 8), (1, 32)))
    return {"pre_norm": pre_norm, "norm_gain": norm_gain, "queries": queries, "keys": keys, "values": values, "head_grad": head_grad, "key_weight": key_weight, "value_weight": value_weight}


epsilon = 1e-06

def heads_backward(query_l, key_l, value_l, grad_l):
    batches, seq_n, target_n, inner = query_l.shape
    source_n = key_l.shape[2]
    head_count = inner // HEAD_DIM
    query_h = query_l.astype(jnp.float32).reshape(batches, seq_n, target_n, head_count, HEAD_DIM)
    key_h = key_l.astype(jnp.float32).reshape(batches, seq_n, source_n, head_count, HEAD_DIM)
    value_h = value_l.astype(jnp.float32).reshape(batches, seq_n, source_n, head_count, HEAD_DIM)
    grad_h = grad_l.astype(jnp.float32).reshape(batches, seq_n, target_n, head_count, HEAD_DIM)
    scores = jnp.einsum('mnthe,mnshe->mnhts', query_h, key_h)
    softmax_w = jax.nn.softmax(scores, axis=-1)
    rounded_w = softmax_w.astype(jnp.bfloat16).astype(jnp.float32)
    value_grad = jnp.einsum('mnhts,mnthe->mnshe', rounded_w, grad_h).astype(jnp.bfloat16)
    slopes = jnp.einsum('mnthe,mnshe->mnhts', grad_h, value_h)
    center = lax.optimization_barrier(jnp.sum(softmax_w * slopes, axis=-1, keepdims=True))
    score_grad = (softmax_w * (slopes - center)).astype(jnp.bfloat16).astype(jnp.float32)
    key_grad = jnp.einsum('mnhts,mnthe->mnshe', score_grad, query_h).astype(jnp.bfloat16)
    query_local = jnp.einsum('mnhts,mnshe->mnthe', score_grad, key_h).astype(jnp.bfloat16)
    return (query_local.reshape(batches, seq_n, target_n, inner), key_grad.reshape(-1, inner), value_grad.reshape(-1, inner))

def reference(pre_norm, norm_gain, queries, keys, values, head_grad, key_weight, value_weight):
    hidden_f = pre_norm.astype(jnp.float32)
    inverse = lax.rsqrt(lax.optimization_barrier(jnp.mean(hidden_f * hidden_f, axis=-1, keepdims=True)) + epsilon)
    memory = (hidden_f * inverse * norm_gain).astype(jnp.bfloat16)
    memory_rows = memory.reshape(-1, D)

    def one_layer(summed, inputs):
        query_l, key_l, value_l, grad_l, key_w, value_w = inputs
        query_local, key_rows, value_rows = heads_backward(query_l, key_l, value_l, grad_l)
        grad_key = jnp.dot(memory_rows.T, key_rows, preferred_element_type=jnp.float32).astype(jnp.bfloat16)
        grad_value = jnp.dot(memory_rows.T, value_rows, preferred_element_type=jnp.float32).astype(jnp.bfloat16)
        returned = jnp.dot(key_rows, key_w.T, preferred_element_type=jnp.float32)
        returned = returned + jnp.dot(value_rows, value_w.T, preferred_element_type=jnp.float32)
        return (summed + returned, (query_local, grad_key, grad_value))
    start_sum = jnp.zeros((memory_rows.shape[0], D), jnp.float32)
    summed, stacked = lax.scan(one_layer, start_sum, (queries, keys, values, head_grad, key_weight, value_weight))
    query_all, grad_keys, grad_values = stacked
    query_grad = jnp.concatenate([query_all[1:], jnp.zeros_like(query_all[:1])], axis=0)
    memory_grad = summed.reshape(hidden_f.shape)
    scaled = norm_gain * memory_grad
    row_mean = lax.optimization_barrier(jnp.mean(hidden_f * scaled, axis=-1, keepdims=True))
    encoder_grad = (inverse * scaled - hidden_f * inverse * inverse * inverse * row_mean).astype(jnp.bfloat16)
    gain_grad = lax.optimization_barrier(jnp.sum((memory_grad * hidden_f * inverse).reshape(-1, D), axis=0))
    return (query_grad, grad_keys, grad_values, encoder_grad, gain_grad)
```

```python
import jax
import jax.numpy as jnp
from jax import lax
from jax.sharding import Mesh, PartitionSpec as P

HEAD_DIM = 64
EPS = 1e-06
BF = jnp.bfloat16
F32 = jnp.float32
SEC = ("y", "zlo")
ZC = ("zhi", "core")


def backward_heads(query_rows, key_rows, value_rows, grad_rows):
    batches, target_n, inner = query_rows.shape
    source_n = key_rows.shape[1]
    head_count = inner // HEAD_DIM
    query_h = query_rows.reshape(batches, target_n, head_count, HEAD_DIM)
    key_h = key_rows.reshape(batches, source_n, head_count, HEAD_DIM)
    value_h = value_rows.reshape(batches, source_n, head_count, HEAD_DIM)
    grad_h = grad_rows.reshape(batches, target_n, head_count, HEAD_DIM)
    scores = jnp.einsum("mshe,mthe->mhst", key_h, query_h, preferred_element_type=F32)
    highest = jnp.max(scores, axis=2, keepdims=True)
    exponent = jnp.exp(scores - highest)
    softmax_w = exponent / jnp.sum(exponent, axis=2, keepdims=True)
    rounded_w = softmax_w.astype(BF)
    slopes = jnp.einsum("mshe,mthe->mhst", value_h, grad_h, preferred_element_type=F32)
    center = jnp.sum(softmax_w * slopes, axis=2, keepdims=True)
    score_grad = (softmax_w * (slopes - center)).astype(BF)
    value_grad = jnp.einsum("mhst,mthe->mshe", rounded_w, grad_h, preferred_element_type=F32)
    key_grad = jnp.einsum("mhst,mthe->mshe", score_grad, query_h, preferred_element_type=F32)
    query_local = jnp.einsum("mhst,mshe->mthe", score_grad, key_h, preferred_element_type=F32)
    return (
        query_local.astype(BF).reshape(batches, target_n, inner),
        key_grad.astype(BF).reshape(batches * source_n, inner),
        value_grad.astype(BF).reshape(batches * source_n, inner),
    )


def body(pre_norm, norm_gain, queries, keys, values, head_grad, key_weight, value_weight):
    batches, _, source_n, features = pre_norm.shape
    rows = batches * source_n
    piece = rows // 8
    inner = queries.shape[-1]
    weights = lax.all_gather(
        jnp.stack([key_weight[0], value_weight[0]]), "x", axis=1, tiled=True
    )
    hidden = pre_norm.astype(F32).reshape(rows, features)
    inverse = lax.rsqrt(jnp.mean(hidden * hidden, axis=-1, keepdims=True) + EPS)
    memory = (hidden * inverse * norm_gain).astype(BF)
    split = memory.reshape(rows, 4, 4, 2, 128).transpose(1, 3, 0, 2, 4).reshape(8, rows, 512)
    columns = lax.all_to_all(split, ZC, split_axis=0, concat_axis=0, tiled=True)
    columns = columns.reshape(8 * rows, 512)

    query_local, key_grad, value_grad = backward_heads(
        queries[0, :, 0], keys[0, :, 0], values[0, :, 0], head_grad[0, :, 0]
    )
    value_all = lax.all_gather(value_grad, ZC, axis=0, tiled=True)
    key_all = lax.all_gather(key_grad, ZC, axis=0, tiled=True)
    returned = jnp.einsum("rh,dh->rd", value_all, weights[1], preferred_element_type=F32)
    returned += jnp.einsum("rh,dh->rd", key_all, weights[0], preferred_element_type=F32)
    gain_part = jnp.sum(returned * columns.astype(F32), axis=0)

    def shard(grad_all):
        partial = jnp.einsum("rd,rh->dh", columns, grad_all, preferred_element_type=F32)
        return lax.psum_scatter(partial.astype(BF), "x", scatter_dimension=0, tiled=True)

    grad_value = shard(value_all)
    grad_key = shard(key_all)

    returned = returned.astype(BF).reshape(8, 8, piece, 512).transpose(1, 0, 2, 3)
    layers = lax.all_to_all(returned, SEC, split_axis=0, concat_axis=0, tiled=True)
    summed = jnp.sum(layers.astype(F32), axis=0)
    gain_part = lax.psum(gain_part, "x")
    gain_hi = gain_part.astype(BF)
    gain_lo = (gain_part - gain_hi.astype(F32)).astype(BF)
    gain_rows = jnp.broadcast_to(jnp.stack([gain_hi, gain_lo])[None], (8, 2, 512))
    sent = jnp.concatenate([summed.astype(BF), gain_rows], axis=1)
    own = lax.all_to_all(sent, ZC, split_axis=0, concat_axis=0, tiled=True)
    own = own.reshape(4, 2, piece + 2, 4, 128).transpose(2, 0, 3, 1, 4).reshape(piece + 2, features)
    rank = lax.axis_index(SEC)
    my_hidden = lax.dynamic_slice_in_dim(hidden, rank * piece, piece, 0)
    my_inverse = lax.dynamic_slice_in_dim(inverse, rank * piece, piece, 0)
    scaled = norm_gain * own[:piece].astype(F32)
    row_mean = jnp.mean(my_hidden * scaled, axis=-1, keepdims=True)
    mine = my_inverse * scaled - my_hidden * my_inverse * my_inverse * my_inverse * row_mean
    packed = jnp.concatenate([mine.astype(BF), own[piece:]], axis=0)
    everyone = lax.all_to_all(
        jnp.broadcast_to(packed[None], (8,) + packed.shape), SEC, split_axis=0, concat_axis=0, tiled=True
    )
    encoder_grad = everyone[:, :piece].reshape(pre_norm.shape)
    gain_grad = jnp.sum(everyone[:, piece:].astype(F32), axis=(0, 1)) / norm_gain

    order = [(s, s - 1) for s in range(1, 8)]
    query_grad = lax.ppermute(query_local.reshape(queries.shape), SEC, order)
    return (query_grad, grad_key[None], grad_value[None], encoder_grad, gain_grad)


def solution(mesh):
    grid = Mesh(mesh.devices.reshape(4, 2, 4, 4, 2), ("y", "zlo", "zhi", "x", "core"))
    dp = ("zhi", "x", "core")
    return jax.shard_map(
        body,
        mesh=grid,
        in_specs=(
            P(None, dp, None, None),
            P(),
            P(SEC, None, dp, None, None),
            P(SEC, None, dp, None, None),
            P(SEC, None, dp, None, None),
            P(SEC, None, dp, None, None),
            P(SEC, dp, None),
            P(SEC, dp, None),
        ),
        out_specs=(
            P(SEC, None, dp, None, None),
            P(SEC, dp, None),
            P(SEC, dp, None),
            P(None, dp, None, None),
            P(),
        ),
        check_vma=False,
    )
```

```python
import functools

import jax
import jax.numpy as jnp
from jax import lax
from jax.experimental import pallas as pl
from jax.experimental.pallas import tpu as pltpu
from jax.sharding import Mesh, PartitionSpec as P

EPS = 1e-06
BF = jnp.bfloat16
F32 = jnp.float32
SEC = ("y", "zlo")
ZC = ("zhi", "core")
SRC = 48
D = 4096
HD = 2048
COLS = 512
PIECE = 6
VMEM = pl.BlockSpec(memory_space=pltpu.VMEM)
HBM = pl.BlockSpec(memory_space=pl.ANY)
SMEM = pl.BlockSpec(memory_space=pltpu.SMEM)


def shape(dims, dtype=BF):
    return jax.ShapeDtypeStruct(dims, dtype)


def params(mib=32):
    return pltpu.CompilerParams(vmem_limit_bytes=mib * 2**20)


def cost(flops, size):
    return pl.CostEstimate(flops=flops, bytes_accessed=size, transcendentals=0)


def rows_dot(a, b):
    return lax.dot_general(a, b, (((1,), (1,)), ((), ())), preferred_element_type=F32)


def columns_dot(a, b):
    return lax.dot_general(a, b, (((0,), (0,)), ((), ())), preferred_element_type=F32)


def heads_kernel(q_ref, k_ref, v_ref, g_ref, local_ref, grads_ref):
    src = k_ref.shape[0]
    lane = lax.broadcasted_iota(jnp.int32, (src, 256), 1) // 64
    masks = [lane == h for h in range(4)]

    def spread(block):
        zero = jnp.zeros_like(block)
        return jnp.concatenate([jnp.where(m, block, zero) for m in masks], axis=0)

    def diagonal(wide):
        out = wide[:src]
        for h in range(1, 4):
            out = jnp.where(masks[h], wide[h * src : (h + 1) * src], out)
        return out

    for part in range(HD // 256):
        at = pl.ds(part * 256, 256)
        q, g = q_ref[:, at], g_ref[:, at]
        k, v = spread(k_ref[:, at]), spread(v_ref[:, at])
        scores = rows_dot(k, q).reshape(4, src, -1)
        exponent = jnp.exp(scores - jnp.max(scores, axis=1, keepdims=True))
        probs = exponent * (1.0 / jnp.sum(exponent, axis=1, keepdims=True))
        slopes = rows_dot(v, g).reshape(4, src, -1)
        center = jnp.sum(probs * slopes, axis=1, keepdims=True)
        score_grad = (probs * (slopes - center)).astype(BF).reshape(4 * src, -1)
        probs = probs.astype(BF).reshape(4 * src, -1)
        value = jnp.dot(probs, g, preferred_element_type=F32)
        key = jnp.dot(score_grad, q, preferred_element_type=F32)
        grads_ref[:, at] = diagonal(key).astype(BF)
        grads_ref[:, pl.ds(HD + part * 256, 256)] = diagonal(value).astype(BF)
        local_ref[:, at] = columns_dot(score_grad, k).astype(BF)


def heads(q, k, v, g, m):
    tgt = q.shape[3]

    def row(n):
        return pl.BlockSpec((None, None, None, n, HD), lambda i: (0, m, 0, 0, 0))

    return pl.pallas_call(
        heads_kernel,
        grid=(1,),
        in_specs=[row(tgt), row(SRC), row(SRC), row(tgt)],
        out_specs=[pl.BlockSpec((tgt, HD), lambda i: (0, 0)), pl.BlockSpec((SRC, D), lambda i: (0, 0))],
        out_shape=[shape((tgt, HD)), shape((SRC, D))],
        compiler_params=params(),
        cost_estimate=cost(2 * 10**9, 3 * 10**6),
        name="heads",
    )(q, k, v, g)


def memory_kernel(pre_ref, gain_ref, out_ref):
    hidden = pre_ref[...].astype(F32)
    inverse = lax.rsqrt(jnp.mean(hidden * hidden, axis=-1, keepdims=True) + EPS)
    memory = (hidden * inverse * gain_ref[...]).astype(BF)
    for z in range(4):
        for c in range(2):
            for x in range(4):
                start = ((z * 4 + x) * 2 + c) * 128
                out_ref[z * 2 + c, :, x * 128 : (x + 1) * 128] = memory[:, start : start + 128]


def memory_blocks(pre, gain):
    rows = pre.shape[0]
    return pl.pallas_call(
        memory_kernel,
        in_specs=[VMEM, VMEM],
        out_specs=VMEM,
        out_shape=shape((8, rows, COLS)),
        compiler_params=params(),
        cost_estimate=cost(4 * 10**6, 2 * 10**6),
        name="memory",
    )(pre, gain)


def token_blocks(place_ref):
    z, c = place_ref[0], place_ref[1]
    index = []
    for core in (c, 1 - c):
        for step in (0, 3, 1, 2):
            index.append(lax.rem(z + step, 4) * 2 + core)
    return index


def return_kernel(m, place_ref, *refs):
    grads, keys, values = refs[:8], refs[8:12], refs[12:16]
    cols_ref, out_ref, gain_ref, grad_s, weight_s, cols_s, acc_s, sems = refs[16:]
    x = place_ref[2]
    copies = []
    for r in range(4):
        at = lax.rem(x + r, 4)
        copies.append((keys[r], weight_s.at[at, :, pl.ds(0, HD)]))
        copies.append((values[r], weight_s.at[at, :, pl.ds(HD, HD)]))
    for ref, zc in zip(grads, token_blocks(place_ref)):
        copies.append((ref, grad_s.at[zc]))
    copies.append((cols_ref.at[:, m], cols_s))
    copies = [pltpu.make_async_copy(a, b, sems.at[i]) for i, (a, b) in enumerate(copies)]
    for copy in copies:
        copy.start()
    for copy in copies:
        copy.wait()
    grad = grad_s[...].reshape(8 * SRC, D)
    for n in range(2):
        weight = weight_s[pl.ds(2 * n, 2)].reshape(256, D)
        acc_s[:, pl.ds(256 * n, 256)] = rows_dot(grad, weight)
    result = acc_s[...]
    columns = cols_s[...].reshape(8 * SRC, COLS).astype(F32)
    gain = jnp.sum(result * columns, axis=0, keepdims=True)
    gain_ref[...] = jnp.broadcast_to(gain, gain_ref.shape)
    rows = 8 * SRC
    target = lax.broadcasted_iota(jnp.int32, (rows, rows), 0)
    source = lax.broadcasted_iota(jnp.int32, (rows, rows), 1)
    rank, rest = target // SRC, target % SRC
    wanted = (rest // PIECE) * SRC + rank * PIECE + rest % PIECE
    move = (source == wanted).astype(F32).astype(BF)
    moved = jnp.dot(move, result.astype(BF), preferred_element_type=F32)
    out_ref[...] = moved.astype(BF).reshape(8, SRC, COLS)


def return_blocks(m, place, grads, keys, values, columns):
    return pl.pallas_call(
        functools.partial(return_kernel, m),
        in_specs=[SMEM] + [HBM] * 17,
        out_specs=[VMEM, VMEM],
        out_shape=[shape((8, SRC, COLS)), shape((8, COLS), F32)],
        scratch_shapes=[
            pltpu.VMEM((8, SRC, D), BF),
            pltpu.VMEM((4, 128, D), BF),
            pltpu.VMEM((8, SRC, COLS), BF),
            pltpu.VMEM((8 * SRC, COLS), F32),
            pltpu.SemaphoreType.DMA((17,)),
        ],
        compiler_params=params(),
        cost_estimate=cost(2 * 384 * 4096 * 512, 8 * 10**6),
        name="returned",
    )(place, *grads, *keys, *values, columns)


def weight_kernel(place_ref, *refs):
    grads, cols_ref, outs = refs[:16], refs[16], refs[17:25]
    grad_s, cols_s, sems = refs[25:]
    x = place_ref[2]
    copies = []
    for r in range(4):
        at = pl.ds(pl.multiple_of(lax.rem(x + r, 4) * 128, 128), 128)
        for m in range(2):
            copies.append((cols_ref.at[:, m, :, at], cols_s.at[m, :, :, pl.ds(r * 128, 128)]))
    blocks = token_blocks(place_ref)
    for m in range(2):
        for i, zc in enumerate(blocks):
            copies.append((grads[8 * m + i], grad_s.at[m, zc]))
    copies = [pltpu.make_async_copy(a, b, sems.at[i]) for i, (a, b) in enumerate(copies)]
    for copy in copies:
        copy.start()
    for copy in copies:
        copy.wait()
    columns = cols_s[...].reshape(16 * SRC, COLS)
    for half in range(2):
        for n in range(HD // 512):
            grad = grad_s[:, :, :, pl.ds(half * HD + n * 512, 512)].reshape(16 * SRC, 512)
            partial = columns_dot(columns, grad).astype(BF)
            for r in range(4):
                outs[half * 4 + r][:, pl.ds(n * 512, 512)] = partial[r * 128 : (r + 1) * 128]


def weight_blocks(place, grads, columns):
    return pl.pallas_call(
        weight_kernel,
        in_specs=[SMEM] + [HBM] * 17,
        out_specs=[VMEM] * 8,
        out_shape=[shape((128, HD))] * 8,
        scratch_shapes=[
            pltpu.VMEM((2, 8, SRC, D), BF),
            pltpu.VMEM((2, 8, SRC, COLS), BF),
            pltpu.SemaphoreType.DMA((24,)),
        ],
        compiler_params=params(),
        cost_estimate=cost(2 * 768 * 4096 * 512, 11 * 10**6),
        name="weights",
    )(place, *grads, columns)


def sum_kernel(layers_ref, gains_ref, out_ref):
    total = jnp.sum(layers_ref[...].astype(F32), axis=0).astype(BF)
    target = lax.broadcasted_iota(jnp.int32, (64, SRC), 0)
    source = lax.broadcasted_iota(jnp.int32, (64, SRC), 1)
    wanted = (target // 8) * PIECE + target % 8
    move = ((source == wanted) & (target % 8 < PIECE)).astype(F32).astype(BF)
    moved = jnp.dot(move, total, preferred_element_type=F32)
    gain = jnp.sum(gains_ref[...], axis=0, keepdims=True)
    high = gain.astype(BF).astype(F32)
    row = lax.broadcasted_iota(jnp.int32, (64, COLS), 0) % 8
    moved = jnp.where(row == 6, high, jnp.where(row == 7, gain - high, moved))
    out_ref[...] = moved.astype(BF).reshape(8, 8, COLS)


def sum_layers(layers, gains):
    return pl.pallas_call(
        sum_kernel,
        in_specs=[VMEM, VMEM],
        out_specs=VMEM,
        out_shape=shape((8, 8, COLS)),
        compiler_params=params(),
        cost_estimate=cost(4 * 10**6, 10**6),
        name="layers",
    )(layers, gains)


def encoder_kernel(place_ref, own_ref, pre_ref, gain_ref, out_ref, full_s):
    for z in range(4):
        for c in range(2):
            for x in range(4):
                start = ((z * 4 + x) * 2 + c) * 128
                full_s[:, start : start + 128] = own_ref[z * 2 + c, :, x * 128 : (x + 1) * 128]
    own = full_s[...].astype(F32)
    target = lax.broadcasted_iota(jnp.int32, (8, SRC), 0)
    source = lax.broadcasted_iota(jnp.int32, (8, SRC), 1)
    pick = ((source == place_ref[3] * PIECE + target) & (target < PIECE)).astype(F32).astype(BF)
    hidden = jnp.dot(pick, pre_ref[...], preferred_element_type=F32)
    inverse = lax.rsqrt(jnp.mean(hidden * hidden, axis=-1, keepdims=True) + EPS)
    scaled = own * gain_ref[...]
    row_mean = jnp.mean(hidden * scaled, axis=-1, keepdims=True)
    mine = inverse * scaled - hidden * (inverse * inverse * inverse * row_mean)
    row = lax.broadcasted_iota(jnp.int32, (8, D), 0)
    packed = jnp.where(row < PIECE, mine, own).astype(BF)
    for s in range(8):
        out_ref[s] = packed


def encoder_rows(place, own, pre, gain, m):
    return pl.pallas_call(
        encoder_kernel,
        grid=(1,),
        in_specs=[
            SMEM,
            pl.BlockSpec((8, 8, COLS), lambda i: (0, 0, 0)),
            pl.BlockSpec((None, None, SRC, D), lambda i: (m, 0, 0, 0)),
            pl.BlockSpec((1, D), lambda i: (0, 0)),
        ],
        out_specs=pl.BlockSpec((8, 8, D), lambda i: (0, 0, 0)),
        out_shape=shape((8, 8, D)),
        scratch_shapes=[pltpu.VMEM((8, D), BF)],
        compiler_params=params(),
        cost_estimate=cost(10**6, 10**6),
        name="encoder",
    )(place, own, pre, gain)


def finish_kernel(first_ref, second_ref, gain_ref, out_ref, gain_out_ref):
    target = lax.broadcasted_iota(jnp.int32, (SRC, 64), 0)
    source = lax.broadcasted_iota(jnp.int32, (SRC, 64), 1)
    wanted = (target // PIECE) * 8 + target % PIECE
    move = (source == wanted).astype(F32).astype(BF)
    for m, ref in enumerate((first_ref, second_ref)):
        packed = ref[...].reshape(64, D)
        out_ref[m, 0] = jnp.dot(move, packed, preferred_element_type=F32).astype(BF)
    row = lax.broadcasted_iota(jnp.int32, (64, D), 0) % 8
    terms = jnp.where(row >= PIECE, second_ref[...].reshape(64, D).astype(F32), 0.0)
    gain_out_ref[...] = jnp.sum(terms, axis=0, keepdims=True) / gain_ref[...]


def finish(first, second, gain):
    return pl.pallas_call(
        finish_kernel,
        in_specs=[VMEM] * 3,
        out_specs=[VMEM, VMEM],
        out_shape=[shape((2, 1, SRC, D)), shape((1, D), F32)],
        compiler_params=params(),
        cost_estimate=cost(10**6, 2 * 10**6),
        name="finish",
    )(first, second, gain)


def shift(value, axis, step):
    return lax.ppermute(value, axis, [(i, (i + step) % 4) for i in range(4)])


def swap(value):
    return lax.ppermute(value, "core", [(0, 1), (1, 0)])


def after(value, *others):
    return lax.optimization_barrier((value,) + others)[0]


def exchange(value, axes):
    return lax.all_to_all(value, axes, split_axis=0, concat_axis=0, tiled=True)


def body(pre_norm, norm_gain, queries, keys, values, head_grad, key_weight, value_weight):
    batches, _, source_n, features = pre_norm.shape
    place = jnp.stack(
        [lax.axis_index("zhi"), lax.axis_index("core"), lax.axis_index("x"), lax.axis_index(SEC)]
    ).astype(jnp.int32)
    gain = norm_gain.reshape(1, features)
    key_w, value_w = key_weight[0], value_weight[0]

    key_m, key_p = shift(key_w, "x", 1), shift(key_w, "x", -1)
    value_m, value_p = shift(value_w, "x", 1), shift(value_w, "x", -1)
    key_2, value_2 = shift(key_m, "x", 1), shift(value_p, "x", -1)
    keys_all = (key_w, key_p, key_2, key_m)
    values_all = (value_w, value_p, value_2, value_m)

    blocks = memory_blocks(pre_norm.reshape(batches * source_n, features), gain)
    columns = exchange(blocks, ZC).reshape(8, batches, source_n, COLS)

    local0, own0 = heads(queries, keys, values, head_grad, 0)
    minus0, plus0 = shift(own0, "zhi", 1), shift(own0, "zhi", -1)
    local1, own1 = heads(queries, keys, values, head_grad, 1)
    far0 = shift(minus0, "zhi", 1)
    plus1 = shift(after(own1, plus0), "zhi", -1)
    minus1 = shift(after(own1, far0), "zhi", 1)
    far1 = shift(plus1, "zhi", -1)
    grads0 = [own0, minus0, plus0, far0]
    grads0 += [swap(v) for v in grads0]
    grads1 = [own1, minus1, plus1, far1]
    grads1 += [swap(v) for v in grads1]

    def encoder(m, returned, gains):
        layers = exchange(returned, SEC)
        own = exchange(sum_layers(layers, gains), ZC)
        return exchange(encoder_rows(place, own, pre_norm, gain, m), SEC)

    returned0, gain0 = return_blocks(0, place, grads0, keys_all, values_all, columns)
    first = encoder(0, returned0, jnp.zeros((4, COLS), F32))
    returned1, gain1 = return_blocks(1, place, grads1, keys_all, values_all, columns)
    gain_part = gain0 + gain1
    gains = jnp.stack([gain_part[0]] + [shift(gain_part, "x", i)[0] for i in (1, 2, 3)])
    second = encoder(1, returned1, gains)

    partial = weight_blocks(place, grads0 + grads1, columns)
    key_part, value_part = partial[:4], partial[4:]

    def add(*terms):
        return sum(t.astype(F32) for t in terms).astype(BF)

    key_far, value_far = shift(key_part[2], "x", 1), shift(value_part[2], "x", -1)
    key_back, value_on = shift(key_part[3], "x", -1), shift(value_part[1], "x", 1)
    key_on = shift(add(key_part[1], key_far), "x", 1)
    value_back = shift(add(value_part[3], value_far), "x", -1)
    grad_key = add(key_part[0], key_on, key_back)
    grad_value = add(value_part[0], value_on, value_back)

    query_local = jnp.stack([local0, local1]).reshape(queries.shape)
    query_grad = lax.ppermute(query_local, SEC, [(s, s - 1) for s in range(1, 8)])
    encoder_grad, gain_grad = finish(first, second, gain)
    return (
        query_grad,
        grad_key[None],
        grad_value[None],
        encoder_grad,
        gain_grad.reshape(features),
    )


def solution(mesh):
    grid = Mesh(mesh.devices.reshape(4, 2, 4, 4, 2), ("y", "zlo", "zhi", "x", "core"))
    dp = ("zhi", "x", "core")
    return jax.shard_map(
        body,
        mesh=grid,
        in_specs=(
            P(None, dp, None, None),
            P(),
            P(SEC, None, dp, None, None),
            P(SEC, None, dp, None, None),
            P(SEC, None, dp, None, None),
            P(SEC, None, dp, None, None),
            P(SEC, dp, None),
            P(SEC, dp, None),
        ),
        out_specs=(
            P(SEC, None, dp, None, None),
            P(SEC, dp, None),
            P(SEC, dp, None),
            P(None, dp, None, None),
            P(),
        ),
        check_vma=False,
    )
```

```python
import functools

import jax
import jax.numpy as jnp
from jax import lax
from jax.experimental import pallas as pl
from jax.experimental.pallas import tpu as pltpu
from jax.sharding import Mesh, PartitionSpec as P

EPS = 1e-06
BF = jnp.bfloat16
F32 = jnp.float32
SEC = ("y", "zlo")
ZC = ("zhi", "core")
SRC = 48
D = 4096
HD = 2048
COLS = 512
PIECE = 6
VMEM = pl.BlockSpec(memory_space=pltpu.VMEM)
HBM = pl.BlockSpec(memory_space=pl.ANY)
SMEM = pl.BlockSpec(memory_space=pltpu.SMEM)


def shape(dims, dtype=BF):
    return jax.ShapeDtypeStruct(dims, dtype)


def params(mib=60):
    return pltpu.CompilerParams(vmem_limit_bytes=mib * 2**20)


def cost(flops, size):
    return pl.CostEstimate(flops=flops, bytes_accessed=size, transcendentals=0)


def rows_dot(a, b):
    return lax.dot_general(a, b, (((1,), (1,)), ((), ())), preferred_element_type=F32)


def columns_dot(a, b):
    return lax.dot_general(a, b, (((0,), (0,)), ((), ())), preferred_element_type=F32)


def heads_kernel(first, q_ref, k_ref, v_ref, g_ref, *refs):
    if first:
        local_ref, grads_ref = refs
        key_out = grads_ref.at[:, pl.ds(0, HD)]
        value_out = grads_ref.at[:, pl.ds(HD, HD)]
    else:
        _, local_ref, key_out, value_out = refs
    src = k_ref.shape[0]
    lane = lax.broadcasted_iota(jnp.int32, (src, 256), 1) // 64
    masks = [lane == h for h in range(4)]

    def spread(block):
        zero = jnp.zeros_like(block)
        return jnp.concatenate([jnp.where(m, block, zero) for m in masks], axis=0)

    def diagonal(wide):
        out = wide[:src]
        for h in range(1, 4):
            out = jnp.where(masks[h], wide[h * src : (h + 1) * src], out)
        return out

    for part in range(HD // 256):
        at = pl.ds(part * 256, 256)
        q, g = q_ref[:, at], g_ref[:, at]
        k, v = spread(k_ref[:, at]), spread(v_ref[:, at])
        scores = rows_dot(k, q).reshape(4, src, -1)
        exponent = jnp.exp(scores - jnp.max(scores, axis=1, keepdims=True))
        probs = exponent * (1.0 / jnp.sum(exponent, axis=1, keepdims=True))
        slopes = rows_dot(v, g).reshape(4, src, -1)
        center = jnp.sum(probs * slopes, axis=1, keepdims=True)
        score_grad = (probs * (slopes - center)).astype(BF).reshape(4 * src, -1)
        probs = probs.astype(BF).reshape(4 * src, -1)
        value = jnp.dot(probs, g, preferred_element_type=F32)
        key = jnp.dot(score_grad, q, preferred_element_type=F32)
        key_out[:, at] = diagonal(key).astype(BF)
        value_out[:, at] = diagonal(value).astype(BF)
        local_ref[:, at] = columns_dot(score_grad, k).astype(BF)


def heads(q, k, v, g, m, local=None):
    tgt = q.shape[3]

    def row(n):
        return pl.BlockSpec((None, None, None, n, HD), lambda i: (0, m, 0, 0, 0))

    def whole(n, w):
        return pl.BlockSpec((n, w), lambda i: (0, 0))

    first = local is None
    grads = [(SRC, D)] if first else [(SRC, HD), (SRC, HD)]
    return pl.pallas_call(
        functools.partial(heads_kernel, first),
        grid=(1,),
        in_specs=[row(tgt), row(SRC), row(SRC), row(tgt)] + ([] if first else [HBM]),
        out_specs=[row(tgt)] + [whole(*dims) for dims in grads],
        out_shape=[shape(q.shape)] + [shape(dims) for dims in grads],
        input_output_aliases={} if first else {4: 0},
        compiler_params=params(),
        cost_estimate=cost(2 * 10**9, 3 * 10**6),
        name="heads",
    )(q, k, v, g, *([] if first else [local]))


def memory_kernel(place_ref, pre_ref, gain_ref, out_ref):
    rows, features = pre_ref.shape
    squares = jnp.zeros((rows, 128), F32)
    for n in range(features // 128):
        part = pre_ref[:, pl.ds(n * 128, 128)].astype(F32)
        squares += part * part
    inverse = lax.rsqrt(jnp.sum(squares, axis=-1, keepdims=True) / features + EPS)
    for z in range(4):
        for c in range(2):
            at = pl.ds(pl.multiple_of(((z * 4 + place_ref[4]) * 2 + c) * 128, 128), 128)
            hidden = pre_ref[:, at].astype(F32)
            out_ref[z * 2 + c] = (hidden * inverse * gain_ref[:, at]).astype(BF)


def memory_blocks(place, pre, gain):
    rows = pre.shape[0]
    return pl.pallas_call(
        memory_kernel,
        in_specs=[SMEM, VMEM, VMEM],
        out_specs=VMEM,
        out_shape=shape((8, rows, 128)),
        compiler_params=params(),
        cost_estimate=cost(4 * 10**6, 2 * 10**6),
        name="memory",
    )(place, pre, gain)


def token_blocks(place_ref):
    z, c = place_ref[0], place_ref[1]
    index = []
    for core in (c, 1 - c):
        for step in (0, 3, 1, 2):
            index.append(lax.rem(z + step, 4) * 2 + core)
    return index


def copy_all(pairs, sems):
    copies = [pltpu.make_async_copy(a, b, sems.at[i]) for i, (a, b) in enumerate(pairs)]
    for copy in copies:
        copy.start()
    for copy in copies:
        copy.wait()


def lanes(index):
    return pl.ds(pl.multiple_of(index * 128, 128), 128)


def return_kernel(m, place_ref, *refs):
    keys, values, cols = refs[:4], refs[4:8], refs[8:12]
    grads = refs[12:-7]
    out_ref, gain_ref, grad_s, weight_s, cols_s, acc_s, sems = refs[-7:]
    x, y = place_ref[2], place_ref[4]
    pairs = []
    for r in range(4):
        at = lax.rem(x + r, 4)
        pairs.append((keys[r], weight_s.at[at, :, pl.ds(0, HD)]))
        pairs.append((values[r], weight_s.at[at, :, pl.ds(HD, HD)]))
        pairs.append((cols[r].at[:, m], cols_s.at[:, :, lanes(lax.rem(y + r, 4))]))
    for i, zc in enumerate(token_blocks(place_ref)):
        if len(grads) == 8:
            pairs.append((grads[i], grad_s.at[zc]))
        else:
            pairs.append((grads[i], grad_s.at[zc, :, pl.ds(0, HD)]))
            pairs.append((grads[8 + i], grad_s.at[zc, :, pl.ds(HD, HD)]))
    copy_all(pairs, sems)
    grad = grad_s[...].reshape(8 * SRC, D)
    for n in range(2):
        weight = weight_s[pl.ds(2 * n, 2)].reshape(256, D)
        acc_s[:, pl.ds(256 * n, 256)] = rows_dot(grad, weight)
    result = acc_s[...]
    columns = cols_s[...].reshape(8 * SRC, COLS).astype(F32)
    gain = jnp.sum(result * columns, axis=0, keepdims=True)
    gain_ref[...] = jnp.broadcast_to(gain, gain_ref.shape)
    rows = 8 * SRC
    target = lax.broadcasted_iota(jnp.int32, (rows, rows), 0)
    source = lax.broadcasted_iota(jnp.int32, (rows, rows), 1)
    rank, rest = target // SRC, target % SRC
    wanted = (rest // PIECE) * SRC + rank * PIECE + rest % PIECE
    move = (source == wanted).astype(F32).astype(BF)
    moved = jnp.dot(move, result.astype(BF), preferred_element_type=F32)
    out_ref[...] = moved.astype(BF).reshape(8, SRC, COLS)


def return_blocks(m, place, keys, values, columns, grads):
    return pl.pallas_call(
        functools.partial(return_kernel, m),
        in_specs=[SMEM] + [HBM] * (12 + len(grads)),
        out_specs=[VMEM, VMEM],
        out_shape=[shape((8, SRC, COLS)), shape((8, COLS), F32)],
        scratch_shapes=[
            pltpu.VMEM((8, SRC, D), BF),
            pltpu.VMEM((4, 128, D), BF),
            pltpu.VMEM((8, SRC, COLS), BF),
            pltpu.VMEM((8 * SRC, COLS), F32),
            pltpu.SemaphoreType.DMA((12 + len(grads),)),
        ],
        compiler_params=params(),
        cost_estimate=cost(2 * 384 * 4096 * 512, 8 * 10**6),
        name="returned",
    )(place, *keys, *values, *columns, *grads)


def weight_kernel(half, place_ref, *refs):
    cols, both, single, outs = refs[:4], refs[4:12], refs[12:20], refs[20:24]
    grad_s, cols_s, sems = refs[24:]
    x, y = place_ref[2], place_ref[4]
    pairs = []
    for r in range(4):
        at = lanes(lax.rem(y + r + 4 - x, 4))
        for m in range(2):
            pairs.append((cols[r].at[:, m], cols_s.at[m, :, :, at]))
    for i, zc in enumerate(token_blocks(place_ref)):
        pairs.append((both[i].at[:, pl.ds(half * HD, HD)], grad_s.at[0, zc]))
        pairs.append((single[i], grad_s.at[1, zc]))
    copy_all(pairs, sems)
    columns = cols_s[...].reshape(16 * SRC, COLS)
    for n in range(HD // 512):
        at = pl.ds(n * 512, 512)
        grad = grad_s[:, :, :, at].reshape(16 * SRC, 512)
        partial = columns_dot(columns, grad).astype(BF)
        for r in range(4):
            outs[r][:, at] = partial[r * 128 : (r + 1) * 128]


def weight_blocks(half, place, columns, both, single):
    return pl.pallas_call(
        functools.partial(weight_kernel, half),
        in_specs=[SMEM] + [HBM] * 20,
        out_specs=[VMEM] * 4,
        out_shape=[shape((128, HD))] * 4,
        scratch_shapes=[
            pltpu.VMEM((2, 8, SRC, HD), BF),
            pltpu.VMEM((2, 8, SRC, COLS), BF),
            pltpu.SemaphoreType.DMA((24,)),
        ],
        compiler_params=params(),
        cost_estimate=cost(2 * 768 * 2048 * 512, 6 * 10**6),
        name="weights",
    )(place, *columns, *both, *single)


def pick_rows(rows, cols, wanted, keep):
    target = lax.broadcasted_iota(jnp.int32, (rows, cols), 0)
    source = lax.broadcasted_iota(jnp.int32, (rows, cols), 1)
    return ((source == wanted(target)) & keep(target)).astype(F32).astype(BF)


def sum_kernel(first_ref, second_ref, gain0_ref, gain1_ref, gain2_ref, gain3_ref, out_ref):
    moved = jnp.zeros((128, COLS), F32)
    for m, ref in enumerate((first_ref, second_ref)):
        total = jnp.sum(ref[...].astype(F32), axis=0).astype(BF)
        move = pick_rows(
            128,
            SRC,
            lambda t: (t // 16) * PIECE + t % 16 - m * PIECE,
            lambda t: (t % 16 >= m * PIECE) & (t % 16 < (m + 1) * PIECE),
        )
        moved += jnp.dot(move, total, preferred_element_type=F32)
    gain = gain0_ref[...] + gain1_ref[...] + gain2_ref[...] + gain3_ref[...]
    gain = gain[:1]
    high = gain.astype(BF).astype(F32)
    row = lax.broadcasted_iota(jnp.int32, (128, COLS), 0) % 16
    moved = jnp.where(row == 12, high, jnp.where(row == 13, gain - high, moved))
    out_ref[...] = moved.astype(BF).reshape(8, 16, COLS)


def sum_layers(first, second, gains):
    return pl.pallas_call(
        sum_kernel,
        in_specs=[VMEM] * 6,
        out_specs=VMEM,
        out_shape=shape((8, 16, COLS)),
        compiler_params=params(),
        cost_estimate=cost(4 * 10**6, 10**6),
        name="layers",
    )(first, second, *gains)


def encoder_kernel(place_ref, own_ref, pre_ref, gain_ref, out_ref, full_s):
    for z in range(4):
        for c in range(2):
            for x in range(4):
                start = ((z * 4 + x) * 2 + c) * 128
                full_s[:, start : start + 128] = own_ref[z * 2 + c, :, x * 128 : (x + 1) * 128]
    own = full_s[...].astype(F32)
    rank = place_ref[3]
    pick = pick_rows(
        16,
        2 * SRC,
        lambda t: (t // PIECE) * SRC + rank * PIECE + t % PIECE,
        lambda t: t < 2 * PIECE,
    )
    hidden = jnp.dot(pick, pre_ref[...], preferred_element_type=F32)
    inverse = lax.rsqrt(jnp.mean(hidden * hidden, axis=-1, keepdims=True) + EPS)
    scaled = own * gain_ref[...]
    row_mean = jnp.mean(hidden * scaled, axis=-1, keepdims=True)
    mine = inverse * scaled - hidden * (inverse * inverse * inverse * row_mean)
    row = lax.broadcasted_iota(jnp.int32, (16, D), 0)
    packed = jnp.where(row < 2 * PIECE, mine, own).astype(BF)
    for s in range(8):
        out_ref[s] = packed


def encoder_rows(place, own, pre, gain):
    return pl.pallas_call(
        encoder_kernel,
        in_specs=[SMEM, VMEM, VMEM, VMEM],
        out_specs=VMEM,
        out_shape=shape((8, 16, D)),
        scratch_shapes=[pltpu.VMEM((16, D), BF)],
        compiler_params=params(),
        cost_estimate=cost(10**6, 2 * 10**6),
        name="encoder",
    )(place, own, pre, gain)


def finish_kernel(packed_ref, gain_ref, out_ref, gain_out_ref):
    packed = packed_ref[...].reshape(128, D)
    move = pick_rows(
        2 * SRC,
        128,
        lambda t: ((t % SRC) // PIECE) * 16 + (t // SRC) * PIECE + t % PIECE,
        lambda t: t >= 0,
    )
    out_ref[...] = jnp.dot(move, packed, preferred_element_type=F32).astype(BF)
    target = lax.broadcasted_iota(jnp.int32, (16, 128), 1) % 16
    ones = ((target == 12) | (target == 13)).astype(F32).astype(BF)
    gain = jnp.dot(ones, packed, preferred_element_type=F32)
    gain_out_ref[...] = gain[:1] / gain_ref[...]


def finish(packed, gain):
    return pl.pallas_call(
        finish_kernel,
        in_specs=[VMEM] * 2,
        out_specs=[VMEM, VMEM],
        out_shape=[shape((2 * SRC, D)), shape((1, D), F32)],
        compiler_params=params(),
        cost_estimate=cost(10**6, 2 * 10**6),
        name="finish",
    )(packed, gain)


def add_kernel(a_ref, b_ref, c_ref, d_ref, out_ref):
    total = a_ref[...].astype(F32) + b_ref[...].astype(F32)
    total += c_ref[...].astype(F32) + d_ref[...].astype(F32)
    out_ref[...] = total.astype(BF)


def add_blocks(*terms):
    dims = terms[0].shape
    block = pl.BlockSpec((32, dims[1]), lambda i: (i, 0))
    return pl.pallas_call(
        add_kernel,
        grid=(dims[0] // 32,),
        in_specs=[block] * 4,
        out_specs=block,
        out_shape=shape(dims),
        compiler_params=params(),
        cost_estimate=cost(10**6, 3 * 10**6),
        name="add",
    )(*terms)


def shift(value, axis, step):
    return lax.ppermute(value, axis, [(i, (i + step) % 4) for i in range(4)])


def swap(value):
    return lax.ppermute(value, "core", [(0, 1), (1, 0)])


def after(value, *others):
    return lax.optimization_barrier((value,) + others)[0]


def exchange(value, axes):
    return lax.all_to_all(value, axes, split_axis=0, concat_axis=0, tiled=True)


def body(pre_norm, norm_gain, queries, keys, values, head_grad, key_weight, value_weight):
    batches, _, source_n, features = pre_norm.shape
    rows = batches * source_n
    place = jnp.stack(
        [lax.axis_index(name) for name in ("zhi", "core", "x", SEC, "y")]
    ).astype(jnp.int32)
    gain = norm_gain.reshape(1, features)
    hidden = pre_norm.reshape(rows, features)
    key_w, value_w = key_weight[0], value_weight[0]

    local, own0 = heads(queries, keys, values, head_grad, 0)
    minus0, plus0 = shift(own0, "zhi", 1), shift(own0, "zhi", -1)
    local, key1, value1 = heads(queries, keys, values, head_grad, 1, local)

    key_w, value_w = lax.optimization_barrier((key_w, value_w, own0))[:2]
    key_m, value_p = shift(key_w, "x", 1), shift(value_w, "x", -1)
    key_p, value_m = shift(key_w, "x", -1), shift(value_w, "x", 1)

    blocks = memory_blocks(place, hidden, gain)
    quarter = exchange(blocks, ZC).reshape(8, batches, source_n, 128)
    columns = (quarter,) + tuple(shift(quarter, "y", -r) for r in (1, 2, 3))

    far0 = shift(after(minus0, value1, blocks), "zhi", 1)
    value1p = shift(after(value1, plus0, quarter), "zhi", -1)
    key1p = shift(after(key1, value1p), "zhi", -1)
    key_2, value_2 = shift(key_m, "x", 1), shift(value_p, "x", -1)
    keys_all = (key_w, key_p, key_2, key_m)
    values_all = (value_w, value_p, value_2, value_m)
    value1m = shift(after(value1, far0), "zhi", 1)
    value1f = shift(after(value1p, key1p), "zhi", -1)
    key1m = shift(after(key1, value1m), "zhi", 1)
    key1f = shift(after(key1p, value1f), "zhi", -1)

    def both_cores(*blocks):
        return list(blocks) + [swap(v) for v in blocks]

    grads0 = both_cores(own0, minus0, plus0, far0)
    values1 = both_cores(value1, value1m, value1p, value1f)
    keys1 = both_cores(key1, key1m, key1p, key1f)

    returned0, gain0 = return_blocks(0, place, keys_all, values_all, columns, grads0)
    layers0 = exchange(returned0, SEC)
    value_part = weight_blocks(1, place, columns, grads0, values1)
    value_in = [shift(value_part[r], "x", r) for r in (2, 1, 3)]
    returned1, gain1 = return_blocks(1, place, keys_all, values_all, columns, keys1 + values1)
    layers1 = exchange(returned1, SEC)
    gain_part = gain0 + gain1
    gains = [gain_part] + [shift(gain_part, "x", i) for i in (1, 2, 3)]
    key_part = weight_blocks(0, place, columns, grads0, keys1)
    key_in = [shift(key_part[r], "x", r) for r in (2, 1, 3)]

    own = exchange(sum_layers(layers0, layers1, gains), ZC)
    packed = exchange(encoder_rows(place, own, hidden, gain), SEC)

    query_grad = lax.ppermute(after(local, key1f), SEC, [(s, s - 1) for s in range(1, 8)])
    grad_value = add_blocks(value_part[0], *value_in)
    grad_key = add_blocks(key_part[0], *key_in)
    encoder_grad, gain_grad = finish(packed, gain)
    return (
        query_grad,
        grad_key[None],
        grad_value[None],
        encoder_grad.reshape(pre_norm.shape),
        gain_grad.reshape(features),
    )


def solution(mesh):
    grid = Mesh(mesh.devices.reshape(4, 2, 4, 4, 2), ("y", "zlo", "zhi", "x", "core"))
    dp = ("zhi", "x", "core")
    return jax.shard_map(
        body,
        mesh=grid,
        in_specs=(
            P(None, dp, None, None),
            P(),
            P(SEC, None, dp, None, None),
            P(SEC, None, dp, None, None),
            P(SEC, None, dp, None, None),
            P(SEC, None, dp, None, None),
            P(SEC, dp, None),
            P(SEC, dp, None),
        ),
        out_specs=(
            P(SEC, None, dp, None, None),
            P(SEC, dp, None),
            P(SEC, dp, None),
            P(None, dp, None, None),
            P(),
        ),
        check_vma=False,
    )
```

```python
import functools

import jax
import jax.numpy as jnp
from jax import lax
from jax.experimental import pallas as pl
from jax.experimental.pallas import tpu as pltpu
from jax.sharding import Mesh, PartitionSpec as P

EPS = 1e-06
BF = jnp.bfloat16
F32 = jnp.float32
SEC = ("y", "zlo")
ZC = ("zhi", "core")
SRC = 48
D = 4096
HD = 2048
COLS = 512
PIECE = 6
VMEM = pl.BlockSpec(memory_space=pltpu.VMEM)
HBM = pl.BlockSpec(memory_space=pl.ANY)
SMEM = pl.BlockSpec(memory_space=pltpu.SMEM)


def shape(dims, dtype=BF):
    return jax.ShapeDtypeStruct(dims, dtype)


def params(mib=60):
    return pltpu.CompilerParams(vmem_limit_bytes=mib * 2**20)


def cost():
    return pl.CostEstimate(flops=0, bytes_accessed=0, transcendentals=0)


def rows_dot(a, b):
    return lax.dot_general(a, b, (((1,), (1,)), ((), ())), preferred_element_type=F32)


def columns_dot(a, b):
    return lax.dot_general(a, b, (((0,), (0,)), ((), ())), preferred_element_type=F32)


def heads_kernel(first, q_ref, k_ref, v_ref, g_ref, *refs):
    if first:
        key_w, value_w, local_ref, grads_ref, stack_ref, sems = refs
        key_out = grads_ref.at[:, pl.ds(0, HD)]
        value_out = grads_ref.at[:, pl.ds(HD, HD)]
        stacked = [
            pltpu.make_async_copy(w.at[0], stack_ref.at[i], sems.at[i])
            for i, w in enumerate((key_w, value_w))
        ]
        for copy in stacked:
            copy.start()
    else:
        _, local_ref, grads_ref = refs
        key_out, value_out = grads_ref.at[0], grads_ref.at[1]
    src = k_ref.shape[0]
    lane = lax.broadcasted_iota(jnp.int32, (src, 256), 1) // 64
    masks = [lane == h for h in range(4)]

    def spread(block):
        zero = jnp.zeros_like(block)
        return jnp.concatenate([jnp.where(m, block, zero) for m in masks], axis=0)

    def diagonal(wide):
        out = wide[:src]
        for h in range(1, 4):
            out = jnp.where(masks[h], wide[h * src : (h + 1) * src], out)
        return out

    for part in range(HD // 256):
        at = pl.ds(part * 256, 256)
        q, g = q_ref[:, at], g_ref[:, at]
        k, v = spread(k_ref[:, at]), spread(v_ref[:, at])
        scores = rows_dot(k, q).reshape(4, src, -1)
        exponent = jnp.exp(scores - jnp.max(scores, axis=1, keepdims=True))
        probs = exponent * (1.0 / jnp.sum(exponent, axis=1, keepdims=True))
        slopes = rows_dot(v, g).reshape(4, src, -1)
        center = jnp.sum(probs * slopes, axis=1, keepdims=True)
        score_grad = (probs * (slopes - center)).astype(BF).reshape(4 * src, -1)
        probs = probs.astype(BF).reshape(4 * src, -1)
        value = jnp.dot(probs, g, preferred_element_type=F32)
        key = jnp.dot(score_grad, q, preferred_element_type=F32)
        key_out[:, at] = diagonal(key).astype(BF)
        value_out[:, at] = diagonal(value).astype(BF)
        local_ref[:, at] = columns_dot(score_grad, k).astype(BF)
    if first:
        for copy in stacked:
            copy.wait()


def heads(q, k, v, g, m, *others):
    tgt = q.shape[3]

    def row(n):
        return pl.BlockSpec((None, None, None, n, HD), lambda i: (0, m, 0, 0, 0))

    if m == 0:
        grads = pl.BlockSpec((SRC, D), lambda i: (0, 0))
        outs = [(grads, shape((SRC, D))), (HBM, shape((2, 128, HD)))]
        scratch = [pltpu.SemaphoreType.DMA((2,))]
    else:
        grads = pl.BlockSpec((2, SRC, HD), lambda i: (0, 0, 0))
        outs, scratch = [(grads, shape((2, SRC, HD)))], []
    return pl.pallas_call(
        functools.partial(heads_kernel, m == 0),
        grid=(1,),
        in_specs=[row(tgt), row(SRC), row(SRC), row(tgt)] + [HBM] * len(others),
        out_specs=[row(tgt)] + [spec for spec, _ in outs],
        out_shape=[shape(q.shape)] + [struct for _, struct in outs],
        input_output_aliases={} if m == 0 else {4: 0},
        scratch_shapes=scratch,
        compiler_params=params(),
        cost_estimate=cost(),
        name="heads",
    )(q, k, v, g, *others)


def memory_kernel(place_ref, pre_ref, gain_ref, out_ref):
    rows, features = pre_ref.shape
    squares = jnp.zeros((rows, 128), F32)
    for n in range(features // 128):
        part = pre_ref[:, pl.ds(n * 128, 128)].astype(F32)
        squares += part * part
    inverse = lax.rsqrt(jnp.sum(squares, axis=-1, keepdims=True) / features + EPS)
    for z in range(4):
        for c in range(2):
            at = pl.ds(pl.multiple_of(((z * 4 + place_ref[4]) * 2 + c) * 128, 128), 128)
            hidden = pre_ref[:, at].astype(F32)
            out_ref[z * 2 + c] = (hidden * inverse * gain_ref[:, at]).astype(BF)


def memory_blocks(place, pre, gain):
    rows = pre.shape[0]
    return pl.pallas_call(
        memory_kernel,
        in_specs=[SMEM, VMEM, VMEM],
        out_specs=VMEM,
        out_shape=shape((8, rows, 128)),
        compiler_params=params(),
        cost_estimate=cost(),
        name="memory",
    )(place, pre, gain)


def token_blocks(place_ref):
    z, c = place_ref[0], place_ref[1]
    index = []
    for core in (c, 1 - c):
        for step in (0, 3, 1, 2):
            index.append(lax.rem(z + step, 4) * 2 + core)
    return index


def start_all(pairs, sems, first=0):
    copies = [pltpu.make_async_copy(a, b, sems.at[first + i]) for i, (a, b) in enumerate(pairs)]
    for copy in copies:
        copy.start()
    return copies


def wait_all(copies):
    for copy in copies:
        copy.wait()


def lanes(index):
    return pl.ds(pl.multiple_of(index * 128, 128), 128)


def part(ref, where):
    kind, index = where
    if kind == "pair":
        return ref.at[index]
    if kind == "half":
        return ref.at[:, pl.ds(index * HD, HD)]
    return ref


def return_kernel(m, wheres, place_ref, *refs):
    weights, cols, grads = refs[:8], refs[8:12], refs[12:28]
    out_ref, gain_ref, grad_s, weight_s, cols_s, acc_s, out_s, sems = refs[-8:]
    x, y = place_ref[2], place_ref[4]
    place = token_blocks(place_ref)
    pairs = []
    for i, (ref, where) in enumerate(zip(grads, wheres)):
        half, zc = i // 8, place[i % 8]
        pairs.append((part(ref, where), grad_s.at[zc, :, pl.ds(half * HD, HD)]))
    for r in range(4):
        for half in range(2):
            ref = weights[2 * r + half]
            ref = ref.at[half] if len(ref.shape) == 3 else ref
            pairs.append((ref, weight_s.at[r, :, pl.ds(half * HD, HD)]))
    for r in range(4):
        at = lanes(lax.rem(y + r + 4 - x, 4))
        pairs.append((cols[r].at[:, m], cols_s.at[:, :, at]))
    copies = start_all(pairs, sems)
    wait_all(copies[:20])
    grad = grad_s[...].reshape(8 * SRC, D)
    for n in range(2):
        if n == 1:
            wait_all(copies[20:])
        weight = weight_s[pl.ds(2 * n, 2)].reshape(256, D)
        acc_s[:, pl.ds(256 * n, 256)] = rows_dot(grad, weight)
    result = acc_s[...]
    columns = cols_s[...].reshape(8 * SRC, COLS).astype(F32)
    gain = jnp.sum(result * columns, axis=0, keepdims=True)
    for r in range(4):
        block = gain[:, r * 128 : (r + 1) * 128]
        gain_ref[:, lanes(lax.rem(x + r, 4))] = jnp.broadcast_to(block, (8, 128))
    rows = 8 * SRC
    target = lax.broadcasted_iota(jnp.int32, (rows, rows), 0)
    source = lax.broadcasted_iota(jnp.int32, (rows, rows), 1)
    rank, rest = target // SRC, target % SRC
    wanted = (rest // PIECE) * SRC + rank * PIECE + rest % PIECE
    move = (source == wanted).astype(F32).astype(BF)
    moved = jnp.dot(move, result.astype(BF), preferred_element_type=F32)
    out_s[...] = moved.astype(BF).reshape(8, SRC, COLS)
    wait_all(start_all([(out_s, out_ref.at[:, m])], sems))


def return_blocks(m, place, weights, columns, grads, *before):
    refs, wheres = zip(*grads)
    return pl.pallas_call(
        functools.partial(return_kernel, m, wheres),
        in_specs=[SMEM] + [HBM] * (28 + len(before)),
        out_specs=[HBM, VMEM],
        out_shape=[shape((8, 2, SRC, COLS)), shape((8, COLS), F32)],
        input_output_aliases={29: 0} if before else {},
        scratch_shapes=[
            pltpu.VMEM((8, SRC, D), BF),
            pltpu.VMEM((4, 128, D), BF),
            pltpu.VMEM((8, SRC, COLS), BF),
            pltpu.VMEM((8 * SRC, COLS), F32),
            pltpu.VMEM((8, SRC, COLS), BF),
            pltpu.SemaphoreType.DMA((28,)),
        ],
        compiler_params=params(),
        cost_estimate=cost(),
        name="returned",
    )(place, *weights, *columns, *refs, *before)


def weight_kernel(wheres, place_ref, *refs):
    cols, grads, outs = refs[:4], refs[4:20], refs[20:24]
    grad_s, cols_s, sems = refs[24:]
    x, y = place_ref[2], place_ref[4]
    place = token_blocks(place_ref)
    pairs = []
    for r in range(4):
        at = lanes(lax.rem(y + r + 4 - x, 4))
        for m in range(2):
            pairs.append((cols[r].at[:, m], cols_s.at[m, :, :, at]))
    for i, (ref, where) in enumerate(zip(grads, wheres)):
        pairs.append((part(ref, where), grad_s.at[i // 8, place[i % 8]]))
    wait_all(start_all(pairs, sems))
    columns = cols_s[...].reshape(16 * SRC, COLS)
    for n in range(HD // 512):
        at = pl.ds(n * 512, 512)
        grad = grad_s[:, :, :, at].reshape(16 * SRC, 512)
        partial = columns_dot(columns, grad).astype(BF)
        for r in range(4):
            outs[r][:, at] = partial[r * 128 : (r + 1) * 128]


def weight_blocks(place, columns, grads):
    refs, wheres = zip(*grads)
    return pl.pallas_call(
        functools.partial(weight_kernel, wheres),
        in_specs=[SMEM] + [HBM] * 20,
        out_specs=[VMEM] * 4,
        out_shape=[shape((128, HD))] * 4,
        scratch_shapes=[
            pltpu.VMEM((2, 8, SRC, HD), BF),
            pltpu.VMEM((2, 8, SRC, COLS), BF),
            pltpu.SemaphoreType.DMA((24,)),
        ],
        compiler_params=params(),
        cost_estimate=cost(),
        name="weights",
    )(place, *columns, *refs)


def pick_rows(rows, cols, wanted, keep):
    target = lax.broadcasted_iota(jnp.int32, (rows, cols), 0)
    source = lax.broadcasted_iota(jnp.int32, (rows, cols), 1)
    return ((source == wanted(target)) & keep(target)).astype(F32).astype(BF)


def sum_kernel(place_ref, layers_ref, gain0_ref, gain1_ref, out_ref):
    moved = jnp.zeros((128, COLS), F32)
    for m in range(2):
        total = jnp.sum(layers_ref[:, m].astype(F32), axis=0).astype(BF)
        move = pick_rows(
            128,
            SRC,
            lambda t: (t // 16) * PIECE + t % 16 - m * PIECE,
            lambda t: (t % 16 >= m * PIECE) & (t % 16 < (m + 1) * PIECE),
        )
        moved += jnp.dot(move, total, preferred_element_type=F32)
    blocks = [lanes(lax.rem(place_ref[2] + r, 4)) for r in range(4)]
    gain = jnp.concatenate([(gain0_ref[:, at] + gain1_ref[:, at])[:1] for at in blocks], axis=1)
    high = gain.astype(BF).astype(F32)
    row = lax.broadcasted_iota(jnp.int32, (128, COLS), 0) % 16
    moved = jnp.where(row == 12, high, jnp.where(row == 13, gain - high, moved))
    out_ref[...] = moved.astype(BF).reshape(8, 16, COLS)


def sum_layers(place, layers, gains):
    return pl.pallas_call(
        sum_kernel,
        in_specs=[SMEM] + [VMEM] * 3,
        out_specs=VMEM,
        out_shape=shape((8, 16, COLS)),
        compiler_params=params(),
        cost_estimate=cost(),
        name="layers",
    )(place, layers, *gains)


def encoder_kernel(
    place_ref, own_ref, pre_ref, gain_ref, query_ref, out_ref, query_out, full_s, sems
):
    handed = start_all([(query_ref, query_out)], sems)
    for z in range(4):
        for c in range(2):
            for x in range(4):
                at = (z * 4 + lax.rem(place_ref[2] + x, 4)) * 2 + c
                full_s[:, lanes(at)] = own_ref[z * 2 + c, :, x * 128 : (x + 1) * 128]
    own = full_s[...].astype(F32)
    rank = place_ref[3]
    pick = pick_rows(
        16,
        2 * SRC,
        lambda t: (t // PIECE) * SRC + rank * PIECE + t % PIECE,
        lambda t: t < 2 * PIECE,
    )
    hidden = jnp.dot(pick, pre_ref[...], preferred_element_type=F32)
    inverse = lax.rsqrt(jnp.mean(hidden * hidden, axis=-1, keepdims=True) + EPS)
    scaled = own * gain_ref[...]
    row_mean = jnp.mean(hidden * scaled, axis=-1, keepdims=True)
    mine = inverse * scaled - hidden * (inverse * inverse * inverse * row_mean)
    row = lax.broadcasted_iota(jnp.int32, (16, D), 0)
    packed = jnp.where(row < 2 * PIECE, mine, own).astype(BF)
    for s in range(8):
        out_ref[s] = packed
    wait_all(handed)


def encoder_rows(place, own, pre, gain, query):
    return pl.pallas_call(
        encoder_kernel,
        in_specs=[SMEM, VMEM, VMEM, VMEM, HBM],
        out_specs=[VMEM, HBM],
        out_shape=[shape((8, 16, D)), shape(query.shape)],
        scratch_shapes=[pltpu.VMEM((16, D), BF), pltpu.SemaphoreType.DMA((1,))],
        compiler_params=params(),
        cost_estimate=cost(),
        name="encoder",
    )(place, own, pre, gain, query)


def finish_kernel(packed_ref, gain_ref, out_ref, gain_out_ref):
    packed = packed_ref[...].reshape(128, D)
    move = pick_rows(
        2 * SRC,
        128,
        lambda t: ((t % SRC) // PIECE) * 16 + (t // SRC) * PIECE + t % PIECE,
        lambda t: t >= 0,
    )
    out_ref[...] = jnp.dot(move, packed, preferred_element_type=F32).astype(BF)
    target = lax.broadcasted_iota(jnp.int32, (16, 128), 1) % 16
    ones = ((target == 12) | (target == 13)).astype(F32).astype(BF)
    gain = jnp.dot(ones, packed, preferred_element_type=F32)
    gain_out_ref[...] = gain[:1] / gain_ref[...]


def finish(packed, gain):
    return pl.pallas_call(
        finish_kernel,
        in_specs=[VMEM] * 2,
        out_specs=[VMEM, VMEM],
        out_shape=[shape((2 * SRC, D)), shape((1, D), F32)],
        compiler_params=params(),
        cost_estimate=cost(),
        name="finish",
    )(packed, gain)


def add_kernel(a_ref, b_ref, c_ref, d_ref, out_ref, terms_s, sems):
    refs = (a_ref, b_ref, c_ref, d_ref)
    wait_all(start_all([(ref, terms_s.at[i]) for i, ref in enumerate(refs)], sems))
    total = terms_s[0].astype(F32) + terms_s[1].astype(F32)
    total += terms_s[2].astype(F32) + terms_s[3].astype(F32)
    out_ref[...] = total.astype(BF)


def add_blocks(*terms):
    dims = terms[0].shape
    return pl.pallas_call(
        add_kernel,
        in_specs=[HBM] * 4,
        out_specs=VMEM,
        out_shape=shape(dims),
        scratch_shapes=[pltpu.VMEM((4,) + dims, BF), pltpu.SemaphoreType.DMA((4,))],
        compiler_params=params(),
        cost_estimate=cost(),
        name="add",
    )(*terms)


def shift(value, axis, step):
    return lax.ppermute(value, axis, [(i, (i + step) % 4) for i in range(4)])


def swap(value):
    return lax.ppermute(value, "core", [(0, 1), (1, 0)])


def after(value, *others):
    return lax.optimization_barrier((value,) + others)[0]


def exchange(value, axes):
    return lax.all_to_all(value, axes, split_axis=0, concat_axis=0, tiled=True)


class Chain:
    def __init__(self):
        self.last = ()

    def __call__(self, value, move, *others):
        result = move(after(value, *self.last, *others))
        self.last = (result,)
        return result


def body(pre_norm, norm_gain, queries, keys, values, head_grad, key_weight, value_weight):
    batches, _, source_n, features = pre_norm.shape
    rows = batches * source_n
    place = jnp.stack(
        [lax.axis_index(name) for name in ("zhi", "core", "x", SEC, "y")]
    ).astype(jnp.int32)
    gain = norm_gain.reshape(1, features)
    hidden = pre_norm.reshape(rows, features)
    side = Chain()

    local, own0, stacked = heads(queries, keys, values, head_grad, 0, key_weight, value_weight)
    minus0, plus0 = shift(own0, "zhi", 1), shift(own0, "zhi", -1)
    weight_m, weight_p = shift(stacked, "x", 1), shift(stacked, "x", -1)
    own0_s = side(own0, swap)
    local, own1 = heads(after(queries, own0), keys, values, head_grad, 1, local)
    own1_s = side(own1, swap)
    blocks = memory_blocks(place, after(hidden, own1), gain)
    quarter = exchange(blocks, ZC).reshape(8, batches, source_n, 128)
    minus0, plus0, weight_m, weight_p, own1, own1_s, quarter = lax.optimization_barrier(
        (minus0, plus0, weight_m, weight_p, own1, own1_s, quarter)
    )

    far0 = shift(minus0, "zhi", 1)
    plus1 = shift(own1, "zhi", -1)
    key_2, value_2 = shift(weight_m[0], "x", 1), shift(weight_p[1], "x", -1)
    minus0_s = side(minus0, swap)
    quarter = after(quarter, key_2, value_2)
    quarter_p, quarter_2, quarter_m = (shift(quarter, "y", -r) for r in (1, 2, 3))
    far0, plus0, plus1, minus0_s, quarter_p, quarter_2, quarter_m = lax.optimization_barrier(
        (far0, plus0, plus1, minus0_s, quarter_p, quarter_2, quarter_m)
    )
    columns = (quarter, quarter_p, quarter_2, quarter_m)
    weights = (stacked, stacked, weight_p, weight_p, key_2, value_2, weight_m, weight_m)

    value1m = shift(after(own1[1], far0), "zhi", 1)
    value1f = shift(plus1[1], "zhi", -1)
    far0_s, plus0_s, plus1_s = swap(far0), swap(plus0), swap(plus1)
    blocks0 = (own0, minus0, plus0, far0, own0_s, minus0_s, plus0_s, far0_s)
    keys0, values0 = ([(b, ("half", i)) for b in blocks0] for i in range(2))
    returned, gain0 = return_blocks(0, place, weights, columns, keys0 + values0)
    value1m, value1f, returned, plus1_s = lax.optimization_barrier(
        (value1m, value1f, returned, plus1_s)
    )

    key1m = shift(after(own1[0], value1m), "zhi", 1)
    key1f = shift(after(plus1[0], value1f), "zhi", -1)
    value1m_s, value1f_s = swap(value1m), swap(value1f)
    whole = ("whole", 0)

    def second(i, minus, far, minus_s, far_s):
        at = ("pair", i)
        first = [(own1, at), (minus, whole), (plus1, at), (far, whole)]
        return first + [(own1_s, at), (minus_s, whole), (plus1_s, at), (far_s, whole)]

    values1 = second(1, value1m, value1f, value1m_s, value1f_s)
    value_part = weight_blocks(place, columns, values0 + values1)
    value_in = [shift(value_part[r], "x", r) for r in (2, 1, 3)]
    key1m, key1f = lax.optimization_barrier((key1m, key1f, value_part[0]))[:2]

    key1m_s, key1f_s = swap(key1m), swap(key1f)
    keys1 = second(0, key1m, key1f, key1m_s, key1f_s)
    returned, gain1 = return_blocks(1, place, weights, columns, keys1 + values1, returned)
    layers = exchange(returned, SEC)
    query_in = lax.ppermute(
        after(local, key1m_s, key1f_s), SEC, [(s, s - 1) for s in range(1, 8)]
    )
    gain_part = gain0 + gain1
    gain_part += lax.ppermute(gain_part, "x", [(0, 1), (1, 0), (2, 3), (3, 2)])
    gain_other = lax.ppermute(gain_part, "x", [(0, 2), (2, 0), (1, 3), (3, 1)])
    columns = lax.optimization_barrier((*columns, returned))[:4]
    key_part = weight_blocks(place, columns, keys0 + keys1)
    sums = sum_layers(place, after(layers, key_part[0], *value_in), [gain_part, gain_other])
    own = exchange(sums, ZC)
    key_from = lax.optimization_barrier((*key_part, sums, *value_in))[:4]
    key_in = [shift(key_from[r], "x", r) for r in (2, 1, 3)]
    packed, query_grad = encoder_rows(place, own, hidden, gain, query_in)
    packed = exchange(packed, SEC)

    grad_value = add_blocks(value_part[0], *value_in)
    grad_key = add_blocks(key_part[0], *key_in)
    encoder_grad, gain_grad = finish(after(packed, *key_in), gain)
    return (
        query_grad,
        grad_key[None],
        grad_value[None],
        encoder_grad.reshape(pre_norm.shape),
        gain_grad.reshape(features),
    )


def solution(mesh):
    grid = Mesh(mesh.devices.reshape(4, 2, 4, 4, 2), ("y", "zlo", "zhi", "x", "core"))
    dp = ("zhi", "x", "core")
    return jax.shard_map(
        body,
        mesh=grid,
        in_specs=(
            P(None, dp, None, None),
            P(),
            P(SEC, None, dp, None, None),
            P(SEC, None, dp, None, None),
            P(SEC, None, dp, None, None),
            P(SEC, None, dp, None, None),
            P(SEC, dp, None),
            P(SEC, dp, None),
        ),
        out_specs=(
            P(SEC, None, dp, None, None),
            P(SEC, dp, None),
            P(SEC, dp, None),
            P(None, dp, None, None),
            P(),
        ),
        check_vma=False,
    )
```

```python
import functools

import jax
import jax.numpy as jnp
from jax import lax
from jax.experimental import pallas as pl
from jax.experimental.pallas import tpu as pltpu
from jax.sharding import Mesh, PartitionSpec as P

EPS = 1e-06
BF = jnp.bfloat16
F32 = jnp.float32
SEC = ("y", "zlo")
ZC = ("zhi", "core")
SRC = 48
D = 4096
HD = 2048
COLS = 512
PIECE = 6
VMEM = pl.BlockSpec(memory_space=pltpu.VMEM)
HBM = pl.BlockSpec(memory_space=pl.ANY)
PIN = pl.BlockSpec(memory_space=pltpu.HBM)


def shape(dims, dtype=BF):
    return jax.ShapeDtypeStruct(dims, dtype)


def pinned(dims, dtype=BF):
    return pltpu.HBM(dims, dtype)


def hold(*values):
    return [pltpu.with_memory_space_constraint(v, pltpu.HBM) for v in values]


def params(mib=16):
    return pltpu.CompilerParams(vmem_limit_bytes=mib * 2**20)


def cost(megabytes=0):
    return pl.CostEstimate(flops=0, bytes_accessed=megabytes * 2**20, transcendentals=0)


def rows_dot(a, b):
    return lax.dot_general(a, b, (((1,), (1,)), ((), ())), preferred_element_type=F32)


def columns_dot(a, b):
    return lax.dot_general(a, b, (((0,), (0,)), ((), ())), preferred_element_type=F32)


def heads_kernel(first, q_ref, k_ref, v_ref, g_ref, *refs):
    if first:
        key_w, value_w, local_ref, grads_ref, stack_ref = refs
        stack_ref[0], stack_ref[1] = key_w[0], value_w[0]
    else:
        _, local_ref, grads_ref = refs
    key_out = grads_ref.at[:, pl.ds(0, HD)]
    value_out = grads_ref.at[:, pl.ds(HD, HD)]
    src = k_ref.shape[0]
    lane = lax.broadcasted_iota(jnp.int32, (src, 256), 1) // 64
    masks = [lane == h for h in range(4)]

    def spread(block):
        zero = jnp.zeros_like(block)
        return jnp.concatenate([jnp.where(m, block, zero) for m in masks], axis=0)

    def diagonal(wide):
        out = wide[:src]
        for h in range(1, 4):
            out = jnp.where(masks[h], wide[h * src : (h + 1) * src], out)
        return out

    for part in range(HD // 256):
        at = pl.ds(part * 256, 256)
        q, g = q_ref[:, at], g_ref[:, at]
        k, v = spread(k_ref[:, at]), spread(v_ref[:, at])
        scores = rows_dot(k, q).reshape(4, src, -1)
        exponent = jnp.exp(scores - jnp.max(scores, axis=1, keepdims=True))
        probs = exponent * (1.0 / jnp.sum(exponent, axis=1, keepdims=True))
        slopes = rows_dot(v, g).reshape(4, src, -1)
        center = jnp.sum(probs * slopes, axis=1, keepdims=True)
        score_grad = (probs * (slopes - center)).astype(BF).reshape(4 * src, -1)
        probs = probs.astype(BF).reshape(4 * src, -1)
        value = jnp.dot(probs, g, preferred_element_type=F32)
        key = jnp.dot(score_grad, q, preferred_element_type=F32)
        key_out[:, at] = diagonal(key).astype(BF)
        value_out[:, at] = diagonal(value).astype(BF)
        local_ref[:, at] = columns_dot(score_grad, k).astype(BF)


def heads(q, k, v, g, m, *others):
    tgt = q.shape[3]

    def row(n):
        return pl.BlockSpec((None, None, None, n, HD), lambda i: (0, m, 0, 0, 0))

    def whole(*dims):
        return pl.BlockSpec(dims, lambda i: (0,) * len(dims))

    if m == 0:
        outs, more = [(SRC, D), (2, 128, HD)], [whole(1, 128, HD)] * 2
    else:
        outs, more = [(SRC, D)], [HBM]
    return pl.pallas_call(
        functools.partial(heads_kernel, m == 0),
        grid=(1,),
        in_specs=[row(tgt), row(SRC), row(SRC), row(tgt)] + more,
        out_specs=[row(tgt)] + [whole(*dims) for dims in outs],
        out_shape=[shape(q.shape)] + [shape(dims) for dims in outs],
        input_output_aliases={} if m == 0 else {4: 0},
        compiler_params=params(60),
        cost_estimate=cost(40),
        name="heads",
    )(q, k, v, g, *others)


def memory_kernel(pre_ref, gain_ref, out_ref):
    rows, features = pre_ref.shape
    squares = jnp.zeros((rows, 128), F32)
    for n in range(features // 128):
        part = pre_ref[:, pl.ds(n * 128, 128)].astype(F32)
        squares += part * part
    inverse = lax.rsqrt(jnp.sum(squares, axis=-1, keepdims=True) / features + EPS)
    for z in range(4):
        for c in range(2):
            at = pl.ds(pl.multiple_of(((z * 4 + lax.axis_index("y")) * 2 + c) * 128, 128), 128)
            hidden = pre_ref[:, at].astype(F32)
            out_ref[z * 2 + c] = (hidden * inverse * gain_ref[:, at]).astype(BF)


def memory_blocks(pre, gain):
    rows = pre.shape[0]
    return pl.pallas_call(
        memory_kernel,
        in_specs=[VMEM, VMEM],
        out_specs=VMEM,
        out_shape=shape((8, rows, 128)),
        compiler_params=params(60),
        cost_estimate=cost(),
        name="memory",
    )(pre, gain)


def token_blocks():
    z, c = lax.axis_index("zhi"), lax.axis_index("core")
    index = []
    for core in (c, 1 - c):
        for step in (0, 3, 1, 2):
            index.append(lax.rem(z + step, 4) * 2 + core)
    return index


def start_all(pairs, sems, first=0):
    copies = [pltpu.make_async_copy(a, b, sems.at[first + i]) for i, (a, b) in enumerate(pairs)]
    for copy in copies:
        copy.start()
    return copies


def wait_all(copies):
    for copy in copies:
        copy.wait()


def lanes(index):
    return pl.ds(pl.multiple_of(index * 128, 128), 128)


def columns_kernel(*refs):
    cols, out_ref, flip_ref, cols_s, flip_s, sems = refs[:4], *refs[4:]
    x, y = lax.axis_index("x"), lax.axis_index("y")
    pairs = []
    for r in range(4):
        at = lanes(lax.rem(y + r + 4 - x, 4))
        for m in range(2):
            pairs.append((cols[r].at[:, m], cols_s.at[m, :, :, at]))
    wait_all(start_all(pairs, sems))
    columns = cols_s[...].reshape(16 * SRC, COLS)
    kept = start_all([(cols_s, out_ref)], sems)
    for n in range(6):
        at = slice(n * 128, (n + 1) * 128)
        flip_s[:, at] = columns[at].T
    wait_all(kept + start_all([(flip_s, flip_ref)], sems, 1))


def gather_columns(*columns):
    return pl.pallas_call(
        columns_kernel,
        in_specs=[HBM] * 4,
        out_specs=[PIN, PIN],
        out_shape=[pinned((2, 8, SRC, COLS)), pinned((COLS, 16 * SRC))],
        scratch_shapes=[
            pltpu.VMEM((2, 8, SRC, COLS), BF),
            pltpu.VMEM((COLS, 16 * SRC), BF),
            pltpu.SemaphoreType.DMA((8,)),
        ],
        compiler_params=params(),
        cost_estimate=cost(),
        name="columns",
    )(*columns)


def return_kernel(m, *refs):
    weights, grads, refs = refs[:4], refs[4:12], refs[12:]
    if m == 0:
        out_ref, plain_ref, all_ref, grad_s, weight_s, out_s, plain_s, sems = refs
    else:
        cols_ref, before_ref, _, out_ref, gain_ref, all_ref = refs[:6]
        grad_s, weight_s, out_s, plain_s, cols_s, sems = refs[6:]
    x = lax.axis_index("x")
    place = token_blocks()
    pairs = []
    for half in range(2):
        for i, ref in enumerate(grads):
            pairs.append((ref.at[:, pl.ds(half * HD, HD)], grad_s.at[half, place[i]]))
        for r, ref in enumerate(weights):
            pairs.append((ref.at[half], weight_s.at[half, pl.ds(r * 128, 128)]))
    if m == 1:
        pairs += [(cols_ref, cols_s), (before_ref, plain_s)]
    copies = start_all(pairs, sems)
    wait_all(copies[:12])
    result = rows_dot(grad_s[0].reshape(8 * SRC, HD), weight_s[0])
    wait_all(copies[12:])
    kept = start_all([(grad_s, all_ref)], sems)
    result += rows_dot(grad_s[1].reshape(8 * SRC, HD), weight_s[1])
    rounded = result.astype(BF)
    if m == 0:
        plain_s[...] = rounded
        kept += start_all([(plain_s, plain_ref)], sems, 1)
    else:
        first, second = (cols_s[i].reshape(8 * SRC, COLS).astype(F32) for i in range(2))
        gain = jnp.sum(plain_s[...].astype(F32) * first + result * second, axis=0, keepdims=True)
        for r in range(4):
            block = gain[:, r * 128 : (r + 1) * 128]
            gain_ref[:, lanes(lax.rem(x + r, 4))] = jnp.broadcast_to(block, (8, 128))
    rows = 8 * SRC
    target = lax.broadcasted_iota(jnp.int32, (rows, rows), 0)
    source = lax.broadcasted_iota(jnp.int32, (rows, rows), 1)
    rank, rest = target // SRC, target % SRC
    wanted = (rest // PIECE) * SRC + rank * PIECE + rest % PIECE
    move = (source == wanted).astype(F32).astype(BF)
    moved = jnp.dot(move, rounded, preferred_element_type=F32)
    out_s[...] = moved.astype(BF).reshape(8, SRC, COLS)
    wait_all(kept + start_all([(out_s, out_ref.at[:, m])], sems, 2))


def return_blocks(m, weights, grads, *more):
    outs = [pinned((8, 2, SRC, COLS)), pinned((8 * SRC, COLS)), pinned((2, 8, SRC, HD))]
    scratch = [
        pltpu.VMEM((2, 8, SRC, HD), BF),
        pltpu.VMEM((2, COLS, HD), BF),
        pltpu.VMEM((8, SRC, COLS), BF),
        pltpu.VMEM((8 * SRC, COLS), BF),
    ]
    if m == 1:
        outs[1] = shape((8, COLS), F32)
        scratch.append(pltpu.VMEM((2, 8, SRC, COLS), BF))
    return pl.pallas_call(
        functools.partial(return_kernel, m),
        in_specs=[HBM] * 12 + [PIN] * len(more),
        out_specs=[PIN, VMEM if m == 1 else PIN, PIN],
        out_shape=outs,
        input_output_aliases={14: 0} if m == 1 else {},
        scratch_shapes=scratch + [pltpu.SemaphoreType.DMA((26,))],
        compiler_params=params(),
        cost_estimate=cost(),
        name="returned",
    )(*weights, *grads, *hold(*more))


def weight_kernel(flip_ref, first_ref, second_ref, *refs):
    outs, far_p, far_m, grad_s, flip_s, outs_s, sems = refs[:3], *refs[3:]
    kept = []
    pairs = [(flip_ref, flip_s)]
    for half in (1, 0):
        for m, ref in enumerate((first_ref, second_ref)):
            pairs.append((ref.at[half], grad_s.at[half, m]))
    copies = start_all(pairs, sems)
    for half in (1, 0):
        wait_all(copies[:3] if half == 1 else copies[3:])
        for n in range(HD // 512):
            at = pl.ds(n * 512, 512)
            grad = grad_s[half, :, :, :, at].reshape(16 * SRC, 512)
            partial = jnp.dot(flip_s[...], grad, preferred_element_type=F32).astype(BF)
            outs_s[0, half, :, at] = partial[:128]
            outs_s[1, half, :, at] = partial[128:256]
            far_p[half, :, at] = partial[256:320]
            far_m[half, :, at] = partial[320:384]
            outs_s[2, half, :, at] = partial[384:]
        pairs = [(outs_s.at[i, half], out.at[half]) for i, out in enumerate(outs)]
        kept += start_all(pairs, sems, 5 + 3 * half)
    wait_all(kept)


def weight_blocks(flipped, first, second):
    return pl.pallas_call(
        weight_kernel,
        in_specs=[PIN] * 3,
        out_specs=[PIN] * 3 + [VMEM] * 2,
        out_shape=[pinned((2, 128, HD))] * 3 + [shape((2, 64, HD))] * 2,
        scratch_shapes=[
            pltpu.VMEM((2, 2, 8, SRC, HD), BF),
            pltpu.VMEM((COLS, 16 * SRC), BF),
            pltpu.VMEM((3, 2, 128, HD), BF),
            pltpu.SemaphoreType.DMA((11,)),
        ],
        compiler_params=params(),
        cost_estimate=cost(),
        name="weights",
    )(*hold(flipped, first, second))


def relay_kernel(near_p, near_m, far_p, far_m, out_p, out_m, near_s, far_s, sems):
    pairs = [(near_p, near_s.at[0]), (near_m, near_s.at[1])]
    pairs += [(far_p, far_s.at[0]), (far_m, far_s.at[1])]
    wait_all(start_all(pairs, sems))
    first, second = pl.ds(0, 64), pl.ds(64, 64)
    for half in range(2):
        added = near_s[0, half, first].astype(F32) + far_s[0, half].astype(F32)
        out_p[half, first] = added.astype(BF)
        out_p[half, second] = near_s[0, half, second]
        out_m[half, first] = near_s[1, half, first]
        added = near_s[1, half, second].astype(F32) + far_s[1, half].astype(F32)
        out_m[half, second] = added.astype(BF)


def relay_blocks(near_p, near_m, far_p, far_m):
    return pl.pallas_call(
        relay_kernel,
        in_specs=[PIN, PIN, HBM, HBM],
        out_specs=[VMEM] * 2,
        out_shape=[shape(near_p.shape)] * 2,
        scratch_shapes=[
            pltpu.VMEM((2, 2, 128, HD), BF),
            pltpu.VMEM((2, 2, 64, HD), BF),
            pltpu.SemaphoreType.DMA((4,)),
        ],
        compiler_params=params(),
        cost_estimate=cost(),
        name="relay",
    )(*hold(near_p, near_m), far_p, far_m)


def pick_rows(rows, cols, wanted, keep):
    target = lax.broadcasted_iota(jnp.int32, (rows, cols), 0)
    source = lax.broadcasted_iota(jnp.int32, (rows, cols), 1)
    return ((source == wanted(target)) & keep(target)).astype(F32).astype(BF)


def sum_kernel(layers_ref, gain0_ref, gain1_ref, gain2_ref, gain3_ref, out_ref):
    moved = jnp.zeros((128, COLS), F32)
    for m in range(2):
        total = jnp.sum(layers_ref[:, m].astype(F32), axis=0).astype(BF)
        move = pick_rows(
            128,
            SRC,
            lambda t: (t // 16) * PIECE + t % 16 - m * PIECE,
            lambda t: (t % 16 >= m * PIECE) & (t % 16 < (m + 1) * PIECE),
        )
        moved += jnp.dot(move, total, preferred_element_type=F32)
    blocks = [lanes(lax.rem(lax.axis_index("x") + r, 4)) for r in range(4)]
    gains = (gain0_ref, gain1_ref, gain2_ref, gain3_ref)
    gain = jnp.concatenate([sum(ref[:, at] for ref in gains)[:1] for at in blocks], axis=1)
    high = gain.astype(BF).astype(F32)
    row = lax.broadcasted_iota(jnp.int32, (128, COLS), 0) % 16
    moved = jnp.where(row == 12, high, jnp.where(row == 13, gain - high, moved))
    out_ref[...] = moved.astype(BF).reshape(8, 16, COLS)


def sum_layers(layers, gains):
    return pl.pallas_call(
        sum_kernel,
        in_specs=[VMEM] * 5,
        out_specs=VMEM,
        out_shape=shape((8, 16, COLS)),
        compiler_params=params(),
        cost_estimate=cost(),
        name="layers",
    )(layers, *gains)


def encoder_kernel(
    own_ref, pre_ref, gain_ref, out_ref, full_s
):
    for z in range(4):
        for c in range(2):
            for x in range(4):
                at = (z * 4 + lax.rem(lax.axis_index("x") + x, 4)) * 2 + c
                full_s[:, lanes(at)] = own_ref[z * 2 + c, :, x * 128 : (x + 1) * 128]
    own = full_s[...].astype(F32)
    rank = (lax.axis_index("y") * 2 + lax.axis_index("zlo"))
    pick = pick_rows(
        16,
        2 * SRC,
        lambda t: (t // PIECE) * SRC + rank * PIECE + t % PIECE,
        lambda t: t < 2 * PIECE,
    )
    hidden = jnp.dot(pick, pre_ref[...], preferred_element_type=F32)
    inverse = lax.rsqrt(jnp.mean(hidden * hidden, axis=-1, keepdims=True) + EPS)
    scaled = own * gain_ref[...]
    row_mean = jnp.mean(hidden * scaled, axis=-1, keepdims=True)
    mine = inverse * scaled - hidden * (inverse * inverse * inverse * row_mean)
    row = lax.broadcasted_iota(jnp.int32, (16, D), 0)
    packed = jnp.where(row < 2 * PIECE, mine, own).astype(BF)
    for s in range(8):
        out_ref[s] = packed


def encoder_rows(own, pre, gain):
    return pl.pallas_call(
        encoder_kernel,
        in_specs=[VMEM, VMEM, VMEM],
        out_specs=VMEM,
        out_shape=shape((8, 16, D)),
        scratch_shapes=[pltpu.VMEM((16, D), BF)],
        compiler_params=params(),
        cost_estimate=cost(),
        name="encoder",
    )(own, pre, gain)


def finish_kernel(packed_ref, gain_ref, out_ref, gain_out_ref):
    packed = packed_ref[...].reshape(128, D)
    move = pick_rows(
        2 * SRC,
        128,
        lambda t: ((t % SRC) // PIECE) * 16 + (t // SRC) * PIECE + t % PIECE,
        lambda t: t >= 0,
    )
    out_ref[...] = jnp.dot(move, packed, preferred_element_type=F32).astype(BF)
    target = lax.broadcasted_iota(jnp.int32, (16, 128), 1) % 16
    ones = ((target == 12) | (target == 13)).astype(F32).astype(BF)
    gain = jnp.dot(ones, packed, preferred_element_type=F32)
    gain_out_ref[...] = gain[:1] / gain_ref[...]


def finish(packed, gain):
    return pl.pallas_call(
        finish_kernel,
        in_specs=[VMEM, VMEM],
        out_specs=[VMEM, VMEM],
        out_shape=[shape((2 * SRC, D)), shape((1, D), F32)],
        compiler_params=params(),
        cost_estimate=cost(),
        name="finish",
    )(packed, gain)


def add_kernel(*refs):
    terms, (key_out, value_out), (terms_s, sems) = refs[:3], refs[3:5], refs[5:]
    wait_all(start_all([(ref, terms_s.at[i]) for i, ref in enumerate(terms)], sems))
    for half, out in enumerate((key_out, value_out)):
        total = terms_s[0, half].astype(F32) + terms_s[1, half].astype(F32)
        out[...] = (total + terms_s[2, half].astype(F32)).astype(BF)


def add_blocks(*terms):
    dims = terms[0].shape
    return pl.pallas_call(
        add_kernel,
        in_specs=[PIN, HBM, HBM],
        out_specs=[VMEM] * 2,
        out_shape=[shape(dims[1:])] * 2,
        scratch_shapes=[pltpu.VMEM((3,) + dims, BF), pltpu.SemaphoreType.DMA((3,))],
        compiler_params=params(),
        cost_estimate=cost(60),
        name="add",
    )(*hold(terms[0]), *terms[1:])


def hand_kernel(in_ref, out_ref, held_s, sems):
    wait_all(start_all([(in_ref, held_s)], sems))
    wait_all(start_all([(held_s, out_ref)], sems))


def hand_on(value):
    return pl.pallas_call(
        hand_kernel,
        in_specs=[HBM],
        out_specs=PIN,
        out_shape=pinned(value.shape),
        scratch_shapes=[pltpu.VMEM(value.shape, BF), pltpu.SemaphoreType.DMA((1,))],
        compiler_params=params(),
        cost_estimate=cost(80),
        name="hand",
    )(value)


def shift(value, axis, step):
    return lax.ppermute(value, axis, [(i, (i + step) % 4) for i in range(4)])


def swap(value):
    return lax.ppermute(value, "core", [(0, 1), (1, 0)])


def after(value, *others):
    return lax.optimization_barrier((value,) + others)[0]


def exchange(value, axes):
    return lax.all_to_all(value, axes, split_axis=0, concat_axis=0, tiled=True)


class Chain:
    def __init__(self):
        self.last = ()

    def __call__(self, value, move, *others):
        result = move(after(value, *self.last, *others))
        self.last = (result,)
        return result


def body(pre_norm, norm_gain, queries, keys, values, head_grad, key_weight, value_weight):
    batches, _, source_n, features = pre_norm.shape
    rows = batches * source_n
    gain = norm_gain.reshape(1, features)
    hidden = pre_norm.reshape(rows, features)
    side = Chain()

    blocks = memory_blocks(hidden, gain)
    quarter = exchange(blocks, ZC).reshape(8, batches, source_n, 128)
    queries = after(queries, blocks)
    local, own0, stacked = heads(queries, keys, values, head_grad, 0, key_weight, value_weight)
    minus0, plus0 = shift(own0, "zhi", 1), shift(own0, "zhi", -1)
    own0_s = side(own0, swap)
    stacked = after(stacked, own0_s)
    weight_m, weight_p = shift(stacked, "x", 1), shift(stacked, "x", -1)
    local, own1 = heads(after(queries, own0), keys, values, head_grad, 1, local)
    own1_s = side(own1, swap)
    minus0, plus0, weight_m, weight_p, own1, own1_s, quarter = lax.optimization_barrier(
        (minus0, plus0, weight_m, weight_p, own1, own1_s, quarter)
    )

    far0 = shift(minus0, "zhi", 1)
    plus1 = shift(own1, "zhi", -1)
    weight_2 = shift(after(stacked, weight_m), "x", 2)
    minus0_s, plus0_s = swap(minus0), swap(plus0)
    far0, plus1, quarter = lax.optimization_barrier((far0, plus1, quarter))

    minus1 = shift(after(own1, far0), "zhi", 1)
    far1 = shift(plus1, "zhi", -1)
    far0_s, plus1_s = swap(far0), swap(plus1)
    quarters = [quarter] + [shift(quarter, "y", -r) for r in (1, 2, 3)]
    weights = (stacked, weight_p, weight_2, weight_m)
    blocks0 = (own0, minus0, plus0, far0, own0_s, minus0_s, plus0_s, far0_s)
    returned, plain, all0 = return_blocks(0, weights, blocks0)
    columns, flipped = gather_columns(after(quarters[0], returned), *quarters[1:])
    minus1, far1, columns, flipped = lax.optimization_barrier((minus1, far1, columns, flipped))

    minus1_s, far1_s = swap(minus1), swap(far1)
    blocks1 = (own1, minus1, plus1, far1, own1_s, minus1_s, plus1_s, far1_s)
    returned, gain_part, all1 = return_blocks(1, weights, blocks1, columns, plain, returned)
    layers = exchange(returned, SEC)
    query_in = lax.ppermute(
        after(local, layers), SEC, [(s, s - 1) for s in range(1, 8)]
    )
    gains = [gain_part] + [shift(gain_part, "x", r) for r in (1, 2, 3)]
    part = weight_blocks(after(flipped, returned), all0, all1)
    sums = sum_layers(after(layers, part[0]), gains)
    own = exchange(sums, ZC)
    far_p, far_m = lax.optimization_barrier((part[3], part[4], *gains))[:2]
    far_p, far_m = shift(far_p, "x", 1), shift(far_m, "x", -1)
    near_p, near_m = relay_blocks(part[1], part[2], far_p, far_m)
    packed = encoder_rows(after(own, near_p), hidden, gain)
    near_p, near_m = shift(near_p, "x", 1), shift(near_m, "x", -1)
    packed = exchange(packed, SEC)
    grad_key, grad_value = add_blocks(part[0], near_p, near_m)
    query_grad = hand_on(query_in)
    encoder_grad, gain_grad = finish(after(packed, grad_key, query_grad), gain)
    return (
        query_grad,
        grad_key[None],
        grad_value[None],
        encoder_grad.reshape(pre_norm.shape),
        gain_grad.reshape(features),
    )


def solution(mesh):
    grid = Mesh(mesh.devices.reshape(4, 2, 4, 4, 2), ("y", "zlo", "zhi", "x", "core"))
    dp = ("zhi", "x", "core")
    return jax.shard_map(
        body,
        mesh=grid,
        in_specs=(
            P(None, dp, None, None),
            P(),
            P(SEC, None, dp, None, None),
            P(SEC, None, dp, None, None),
            P(SEC, None, dp, None, None),
            P(SEC, None, dp, None, None),
            P(SEC, dp, None),
            P(SEC, dp, None),
        ),
        out_specs=(
            P(SEC, None, dp, None, None),
            P(SEC, dp, None),
            P(SEC, dp, None),
            P(None, dp, None, None),
            P(),
        ),
        check_vma=False,
    )
```

```python
import functools

import jax
import jax.numpy as jnp
from jax import lax
from jax.experimental import pallas as pl
from jax.experimental.pallas import tpu as pltpu
from jax.sharding import Mesh, PartitionSpec as P

EPS = 1e-06
BF = jnp.bfloat16
F32 = jnp.float32
SEC = ("y", "zlo")
ZC = ("zhi", "core")
SRC = 48
D = 4096
HD = 2048
COLS = 512
PIECE = 6
VMEM = pl.BlockSpec(memory_space=pltpu.VMEM)
HBM = pl.BlockSpec(memory_space=pl.ANY)
PIN = pl.BlockSpec(memory_space=pltpu.HBM)


def shape(dims, dtype=BF):
    return jax.ShapeDtypeStruct(dims, dtype)


def pinned(dims, dtype=BF):
    return pltpu.HBM(dims, dtype)


def hold(*values):
    return [pltpu.with_memory_space_constraint(v, pltpu.HBM) for v in values]


def params(mib=16):
    return pltpu.CompilerParams(vmem_limit_bytes=mib * 2**20)


def cost(megabytes=0):
    return pl.CostEstimate(flops=0, bytes_accessed=megabytes * 2**20, transcendentals=0)


def rows_dot(a, b):
    return lax.dot_general(a, b, (((1,), (1,)), ((), ())), preferred_element_type=F32)


def columns_dot(a, b):
    return lax.dot_general(a, b, (((0,), (0,)), ((), ())), preferred_element_type=F32)


def heads_kernel(first, q_ref, k_ref, v_ref, g_ref, *refs):
    if first:
        key_w, value_w, local_ref, grads_ref, stack_ref = refs
        stack_ref[0], stack_ref[1] = key_w[0], value_w[0]
    else:
        _, local_ref, grads_ref = refs
    key_out = grads_ref.at[:, pl.ds(0, HD)]
    value_out = grads_ref.at[:, pl.ds(HD, HD)]
    src = k_ref.shape[0]
    lane = lax.broadcasted_iota(jnp.int32, (src, 256), 1) // 64
    masks = [lane == h for h in range(4)]

    def spread(block):
        zero = jnp.zeros_like(block)
        return jnp.concatenate([jnp.where(m, block, zero) for m in masks], axis=0)

    def diagonal(wide):
        out = wide[:src]
        for h in range(1, 4):
            out = jnp.where(masks[h], wide[h * src : (h + 1) * src], out)
        return out

    for part in range(HD // 256):
        at = pl.ds(part * 256, 256)
        q, g = q_ref[:, at], g_ref[:, at]
        k, v = spread(k_ref[:, at]), spread(v_ref[:, at])
        scores = rows_dot(k, q).reshape(4, src, -1)
        exponent = jnp.exp(scores - jnp.max(scores, axis=1, keepdims=True))
        probs = exponent * (1.0 / jnp.sum(exponent, axis=1, keepdims=True))
        slopes = rows_dot(v, g).reshape(4, src, -1)
        center = jnp.sum(probs * slopes, axis=1, keepdims=True)
        score_grad = (probs * (slopes - center)).astype(BF).reshape(4 * src, -1)
        probs = probs.astype(BF).reshape(4 * src, -1)
        value = jnp.dot(probs, g, preferred_element_type=F32)
        key = jnp.dot(score_grad, q, preferred_element_type=F32)
        key_out[:, at] = diagonal(key).astype(BF)
        value_out[:, at] = diagonal(value).astype(BF)
        local_ref[:, at] = columns_dot(score_grad, k).astype(BF)


def heads(q, k, v, g, m, *others):
    tgt = q.shape[3]

    def row(n):
        return pl.BlockSpec((None, None, None, n, HD), lambda i: (0, m, 0, 0, 0))

    def whole(*dims):
        return pl.BlockSpec(dims, lambda i: (0,) * len(dims))

    if m == 0:
        outs, more = [(SRC, D), (2, 128, HD)], [whole(1, 128, HD)] * 2
    else:
        outs, more = [(SRC, D)], [HBM]
    return pl.pallas_call(
        functools.partial(heads_kernel, m == 0),
        grid=(1,),
        in_specs=[row(tgt), row(SRC), row(SRC), row(tgt)] + more,
        out_specs=[row(tgt)] + [whole(*dims) for dims in outs],
        out_shape=[shape(q.shape)] + [shape(dims) for dims in outs],
        input_output_aliases={} if m == 0 else {4: 0},
        compiler_params=params(60),
        cost_estimate=cost(40),
        name="heads",
    )(q, k, v, g, *others)


def memory_kernel(pre_ref, gain_ref, out_ref):
    rows, features = pre_ref.shape
    squares = jnp.zeros((rows, 128), F32)
    for n in range(features // 128):
        part = pre_ref[:, pl.ds(n * 128, 128)].astype(F32)
        squares += part * part
    inverse = lax.rsqrt(jnp.sum(squares, axis=-1, keepdims=True) / features + EPS)
    for z in range(4):
        for c in range(2):
            at = pl.ds(pl.multiple_of(((z * 4 + lax.axis_index("y")) * 2 + c) * 128, 128), 128)
            hidden = pre_ref[:, at].astype(F32)
            out_ref[z * 2 + c] = (hidden * inverse * gain_ref[:, at]).astype(BF)


def memory_blocks(pre, gain):
    rows = pre.shape[0]
    return pl.pallas_call(
        memory_kernel,
        in_specs=[VMEM, VMEM],
        out_specs=VMEM,
        out_shape=shape((8, rows, 128)),
        compiler_params=params(60),
        cost_estimate=cost(),
        name="memory",
    )(pre, gain)


def token_blocks():
    z, c = lax.axis_index("zhi"), lax.axis_index("core")
    index = []
    for core in (c, 1 - c):
        for step in (0, 3, 1, 2):
            index.append(lax.rem(z + step, 4) * 2 + core)
    return index


def start_all(pairs, sems, first=0):
    copies = [pltpu.make_async_copy(a, b, sems.at[first + i]) for i, (a, b) in enumerate(pairs)]
    for copy in copies:
        copy.start()
    return copies


def wait_all(copies):
    for copy in copies:
        copy.wait()


def lanes(index):
    return pl.ds(pl.multiple_of(index * 128, 128), 128)


def columns_kernel(*refs):
    cols, out_ref, flip_ref, cols_s, flip_s, sems = refs[:4], *refs[4:]
    x, y = lax.axis_index("x"), lax.axis_index("y")
    pairs = []
    for r in range(4):
        at = lanes(lax.rem(y + r + 4 - x, 4))
        for m in range(2):
            pairs.append((cols[r].at[:, m], cols_s.at[m, :, :, at]))
    wait_all(start_all(pairs, sems))
    columns = cols_s[...].reshape(16 * SRC, COLS)
    kept = start_all([(cols_s, out_ref)], sems)
    for n in range(6):
        at = slice(n * 128, (n + 1) * 128)
        flip_s[:, at] = columns[at].T
    wait_all(kept + start_all([(flip_s, flip_ref)], sems, 1))


def gather_columns(*columns):
    return pl.pallas_call(
        columns_kernel,
        in_specs=[HBM] * 4,
        out_specs=[PIN, PIN],
        out_shape=[pinned((2, 8, SRC, COLS)), pinned((COLS, 16 * SRC))],
        scratch_shapes=[
            pltpu.VMEM((2, 8, SRC, COLS), BF),
            pltpu.VMEM((COLS, 16 * SRC), BF),
            pltpu.SemaphoreType.DMA((8,)),
        ],
        compiler_params=params(),
        cost_estimate=cost(),
        name="columns",
    )(*columns)


def return_kernel(m, *refs):
    weights, grads, refs = refs[:4], refs[4:12], refs[12:]
    if m == 0:
        out_ref, plain_ref, all_ref, grad_s, weight_s, out_s, plain_s, sems = refs
    else:
        cols_ref, before_ref, _, out_ref, gain_ref, all_ref = refs[:6]
        grad_s, weight_s, out_s, plain_s, cols_s, sems = refs[6:]
    x = lax.axis_index("x")
    place = token_blocks()
    pairs = []
    for half in range(2):
        for i, ref in enumerate(grads):
            pairs.append((ref.at[:, pl.ds(half * HD, HD)], grad_s.at[half, place[i]]))
        for r, ref in enumerate(weights):
            pairs.append((ref.at[half], weight_s.at[half, pl.ds(r * 128, 128)]))
    if m == 1:
        pairs += [(cols_ref, cols_s), (before_ref, plain_s)]
    copies = start_all(pairs, sems)
    wait_all(copies[:12])
    result = rows_dot(grad_s[0].reshape(8 * SRC, HD), weight_s[0])
    wait_all(copies[12:])
    kept = start_all([(grad_s, all_ref)], sems)
    result += rows_dot(grad_s[1].reshape(8 * SRC, HD), weight_s[1])
    rounded = result.astype(BF)
    if m == 0:
        plain_s[...] = rounded
        kept += start_all([(plain_s, plain_ref)], sems, 1)
    else:
        first, second = (cols_s[i].reshape(8 * SRC, COLS).astype(F32) for i in range(2))
        gain = jnp.sum(plain_s[...].astype(F32) * first + result * second, axis=0, keepdims=True)
        for r in range(4):
            block = gain[:, r * 128 : (r + 1) * 128]
            gain_ref[:, lanes(lax.rem(x + r, 4))] = jnp.broadcast_to(block, (8, 128))
    rows = 8 * SRC
    target = lax.broadcasted_iota(jnp.int32, (rows, rows), 0)
    source = lax.broadcasted_iota(jnp.int32, (rows, rows), 1)
    rank, rest = target // SRC, target % SRC
    wanted = (rest // PIECE) * SRC + rank * PIECE + rest % PIECE
    move = (source == wanted).astype(F32).astype(BF)
    moved = jnp.dot(move, rounded, preferred_element_type=F32)
    out_s[...] = moved.astype(BF).reshape(8, SRC, COLS)
    wait_all(kept + start_all([(out_s, out_ref.at[:, m])], sems, 2))


def return_blocks(m, weights, grads, *more):
    outs = [pinned((8, 2, SRC, COLS)), pinned((8 * SRC, COLS)), pinned((2, 8, SRC, HD))]
    scratch = [
        pltpu.VMEM((2, 8, SRC, HD), BF),
        pltpu.VMEM((2, COLS, HD), BF),
        pltpu.VMEM((8, SRC, COLS), BF),
        pltpu.VMEM((8 * SRC, COLS), BF),
    ]
    if m == 1:
        outs[1] = shape((8, COLS), F32)
        scratch.append(pltpu.VMEM((2, 8, SRC, COLS), BF))
    return pl.pallas_call(
        functools.partial(return_kernel, m),
        in_specs=[HBM] * 12 + [PIN] * len(more),
        out_specs=[PIN, VMEM if m == 1 else PIN, PIN],
        out_shape=outs,
        input_output_aliases={14: 0} if m == 1 else {},
        scratch_shapes=scratch + [pltpu.SemaphoreType.DMA((26,))],
        compiler_params=params(),
        cost_estimate=cost(),
        name="returned",
    )(*weights, *grads, *hold(*more))


def weight_kernel(flip_ref, first_ref, second_ref, *refs):
    outs, far_p, far_m, grad_s, flip_s, outs_s, sems = refs[:3], *refs[3:]
    kept = []
    pairs = [(flip_ref, flip_s)]
    for half in (1, 0):
        for m, ref in enumerate((first_ref, second_ref)):
            pairs.append((ref.at[half], grad_s.at[half, m]))
    copies = start_all(pairs, sems)
    for half in (1, 0):
        wait_all(copies[:3] if half == 1 else copies[3:])
        for n in range(HD // 512):
            at = pl.ds(n * 512, 512)
            grad = grad_s[half, :, :, :, at].reshape(16 * SRC, 512)
            partial = jnp.dot(flip_s[...], grad, preferred_element_type=F32).astype(BF)
            outs_s[0, half, :, at] = partial[:128]
            outs_s[1, half, :, at] = partial[128:256]
            far_p[half, :, at] = partial[256:320]
            far_m[half, :, at] = partial[320:384]
            outs_s[2, half, :, at] = partial[384:]
        pairs = [(outs_s.at[i, half], out.at[half]) for i, out in enumerate(outs)]
        kept += start_all(pairs, sems, 5 + 3 * half)
    wait_all(kept)


def weight_blocks(flipped, first, second):
    return pl.pallas_call(
        weight_kernel,
        in_specs=[PIN] * 3,
        out_specs=[PIN] * 3 + [VMEM] * 2,
        out_shape=[pinned((2, 128, HD))] * 3 + [shape((2, 64, HD))] * 2,
        scratch_shapes=[
            pltpu.VMEM((2, 2, 8, SRC, HD), BF),
            pltpu.VMEM((COLS, 16 * SRC), BF),
            pltpu.VMEM((3, 2, 128, HD), BF),
            pltpu.SemaphoreType.DMA((11,)),
        ],
        compiler_params=params(),
        cost_estimate=cost(),
        name="weights",
    )(*hold(flipped, first, second))


def relay_kernel(near_p, near_m, far_p, far_m, out_p, out_m, near_s, far_s, sems):
    pairs = [(near_p, near_s.at[0]), (near_m, near_s.at[1])]
    pairs += [(far_p, far_s.at[0]), (far_m, far_s.at[1])]
    wait_all(start_all(pairs, sems))
    first, second = pl.ds(0, 64), pl.ds(64, 64)
    for half in range(2):
        added = near_s[0, half, first].astype(F32) + far_s[0, half].astype(F32)
        out_p[half, first] = added.astype(BF)
        out_p[half, second] = near_s[0, half, second]
        out_m[half, first] = near_s[1, half, first]
        added = near_s[1, half, second].astype(F32) + far_s[1, half].astype(F32)
        out_m[half, second] = added.astype(BF)


def relay_blocks(near_p, near_m, far_p, far_m):
    return pl.pallas_call(
        relay_kernel,
        in_specs=[PIN, PIN, HBM, HBM],
        out_specs=[VMEM] * 2,
        out_shape=[shape((2, 128, HD))] * 2,
        scratch_shapes=[
            pltpu.VMEM((2, 2, 128, HD), BF),
            pltpu.VMEM((2, 2, 64, HD), BF),
            pltpu.SemaphoreType.DMA((4,)),
        ],
        compiler_params=params(),
        cost_estimate=cost(),
        name="relay",
    )(*hold(near_p, near_m), far_p, far_m)


def pick_rows(rows, cols, wanted, keep):
    target = lax.broadcasted_iota(jnp.int32, (rows, cols), 0)
    source = lax.broadcasted_iota(jnp.int32, (rows, cols), 1)
    return ((source == wanted(target)) & keep(target)).astype(F32).astype(BF)


def sum_kernel(layers_ref, gain0_ref, gain1_ref, gain2_ref, gain3_ref, out_ref):
    moved = jnp.zeros((128, COLS), F32)
    for m in range(2):
        total = jnp.sum(layers_ref[:, m].astype(F32), axis=0).astype(BF)
        move = pick_rows(
            128,
            SRC,
            lambda t: (t // 16) * PIECE + t % 16 - m * PIECE,
            lambda t: (t % 16 >= m * PIECE) & (t % 16 < (m + 1) * PIECE),
        )
        moved += jnp.dot(move, total, preferred_element_type=F32)
    blocks = [lanes(lax.rem(lax.axis_index("x") + r, 4)) for r in range(4)]
    gains = (gain0_ref, gain1_ref, gain2_ref, gain3_ref)
    gain = jnp.concatenate([sum(ref[:, at] for ref in gains)[:1] for at in blocks], axis=1)
    high = gain.astype(BF).astype(F32)
    row = lax.broadcasted_iota(jnp.int32, (128, COLS), 0) % 16
    moved = jnp.where(row == 12, high, jnp.where(row == 13, gain - high, moved))
    out_ref[...] = moved.astype(BF).reshape(8, 16, COLS)


def sum_layers(layers, gains):
    return pl.pallas_call(
        sum_kernel,
        in_specs=[VMEM] * 5,
        out_specs=VMEM,
        out_shape=shape((8, 16, COLS)),
        compiler_params=params(),
        cost_estimate=cost(),
        name="layers",
    )(layers, *gains)


def encoder_kernel(
    own_ref, pre_ref, gain_ref, out_ref, full_s
):
    for z in range(4):
        for c in range(2):
            for x in range(4):
                at = (z * 4 + lax.rem(lax.axis_index("x") + x, 4)) * 2 + c
                full_s[:, lanes(at)] = own_ref[z * 2 + c, :, x * 128 : (x + 1) * 128]
    own = full_s[...].astype(F32)
    rank = (lax.axis_index("y") * 2 + lax.axis_index("zlo"))
    pick = pick_rows(
        16,
        2 * SRC,
        lambda t: (t // PIECE) * SRC + rank * PIECE + t % PIECE,
        lambda t: t < 2 * PIECE,
    )
    hidden = jnp.dot(pick, pre_ref[...], preferred_element_type=F32)
    inverse = lax.rsqrt(jnp.mean(hidden * hidden, axis=-1, keepdims=True) + EPS)
    scaled = own * gain_ref[...]
    row_mean = jnp.mean(hidden * scaled, axis=-1, keepdims=True)
    mine = inverse * scaled - hidden * (inverse * inverse * inverse * row_mean)
    row = lax.broadcasted_iota(jnp.int32, (16, D), 0)
    packed = jnp.where(row < 2 * PIECE, mine, own).astype(BF)
    out_ref[...] = packed


def encoder_rows(own, pre, gain):
    return pl.pallas_call(
        encoder_kernel,
        in_specs=[VMEM, VMEM, VMEM],
        out_specs=VMEM,
        out_shape=shape((16, D)),
        scratch_shapes=[pltpu.VMEM((16, D), BF)],
        compiler_params=params(),
        cost_estimate=cost(),
        name="encoder",
    )(own, pre, gain)


def finish_kernel(a_ref, b_ref, c_ref, d_ref, gain_ref, out_ref, gain_out_ref, packed_s, sems):
    y, zlo = lax.axis_index("y"), lax.axis_index("zlo")
    pairs = []
    for r, ref in enumerate((a_ref, b_ref, c_ref, d_ref)):
        for j in range(2):
            rank = lax.rem(y + r, 4) * 2 + (zlo if j == 0 else 1 - zlo)
            pairs.append((ref.at[j], packed_s.at[rank]))
    wait_all(start_all(pairs, sems))
    packed = packed_s[...].reshape(128, D)
    move = pick_rows(
        2 * SRC,
        128,
        lambda t: ((t % SRC) // PIECE) * 16 + (t // SRC) * PIECE + t % PIECE,
        lambda t: t >= 0,
    )
    out_ref[...] = jnp.dot(move, packed, preferred_element_type=F32).astype(BF)
    target = lax.broadcasted_iota(jnp.int32, (16, 128), 1) % 16
    ones = ((target == 12) | (target == 13)).astype(F32).astype(BF)
    gain = jnp.dot(ones, packed, preferred_element_type=F32)
    gain_out_ref[...] = gain[:1] / gain_ref[...]


def finish(packed, gain):
    return pl.pallas_call(
        finish_kernel,
        in_specs=[HBM] * 4 + [VMEM],
        out_specs=[VMEM, VMEM],
        out_shape=[shape((2 * SRC, D)), shape((1, D), F32)],
        scratch_shapes=[pltpu.VMEM((8, 16, D), BF), pltpu.SemaphoreType.DMA((8,))],
        compiler_params=params(),
        cost_estimate=cost(),
        name="finish",
    )(*packed, gain)


def add_kernel(*refs):
    terms, (key_out, value_out), (terms_s, sems) = refs[:3], refs[3:5], refs[5:]
    pairs = [(ref.at[:, pl.ds(0, 128)], terms_s.at[i]) for i, ref in enumerate(terms)]
    wait_all(start_all(pairs, sems))
    for half, out in enumerate((key_out, value_out)):
        total = terms_s[0, half].astype(F32) + terms_s[1, half].astype(F32)
        out[...] = (total + terms_s[2, half].astype(F32)).astype(BF)


def add_blocks(*terms):
    dims = terms[0].shape
    return pl.pallas_call(
        add_kernel,
        in_specs=[PIN, HBM, HBM],
        out_specs=[VMEM] * 2,
        out_shape=[shape(dims[1:])] * 2,
        scratch_shapes=[pltpu.VMEM((3,) + dims, BF), pltpu.SemaphoreType.DMA((3,))],
        compiler_params=params(),
        cost_estimate=cost(400),
        name="add",
    )(*hold(terms[0]), *terms[1:])


def hand_kernel(in_ref, out_ref, held_s, sems):
    wait_all(start_all([(in_ref, held_s)], sems))
    wait_all(start_all([(held_s, out_ref)], sems))


def hand_on(value):
    return pl.pallas_call(
        hand_kernel,
        in_specs=[HBM],
        out_specs=PIN,
        out_shape=pinned(value.shape),
        scratch_shapes=[pltpu.VMEM(value.shape, BF), pltpu.SemaphoreType.DMA((1,))],
        compiler_params=params(),
        cost_estimate=cost(400),
        name="hand",
    )(value)


def shift(value, axis, step):
    return lax.ppermute(value, axis, [(i, (i + step) % 4) for i in range(4)])


def swap(value):
    return lax.ppermute(value, "core", [(0, 1), (1, 0)])


def after(value, *others):
    return lax.optimization_barrier((value,) + others)[0]


def exchange(value, axes):
    return lax.all_to_all(value, axes, split_axis=0, concat_axis=0, tiled=True)


def body(pre_norm, norm_gain, queries, keys, values, head_grad, key_weight, value_weight):
    batches, _, source_n, features = pre_norm.shape
    rows = batches * source_n
    gain = norm_gain.reshape(1, features)
    hidden = pre_norm.reshape(rows, features)

    local, own0, stacked = heads(queries, keys, values, head_grad, 0, key_weight, value_weight)
    minus0, plus0 = shift(own0, "zhi", 1), shift(own0, "zhi", -1)
    own0_s = swap(own0)
    weight_m, weight_p = shift(stacked, "x", 1), shift(stacked, "x", -1)
    blocks = memory_blocks(after(hidden, own0), gain)
    quarter = exchange(blocks, ZC).reshape(8, batches, source_n, 128)
    local, own1 = heads(after(queries, blocks), keys, values, head_grad, 1, local)
    minus0, plus0, weight_m, weight_p, own1, own0_s, quarter = lax.optimization_barrier(
        (minus0, plus0, weight_m, weight_p, own1, own0_s, quarter)
    )

    far0 = shift(minus0, "zhi", 1)
    plus1 = shift(own1, "zhi", -1)
    weight_2 = shift(after(stacked, weight_m), "x", 2)
    minus0_s, plus0_s, own1_s = swap(minus0), swap(plus0), swap(own1)
    far0, plus1, quarter = lax.optimization_barrier((far0, plus1, quarter))

    minus1 = shift(after(own1, far0), "zhi", 1)
    far1 = shift(plus1, "zhi", -1)
    far0_s, plus1_s = swap(far0), swap(plus1)
    quarters = [quarter] + [shift(quarter, "y", -r) for r in (1, 2, 3)]
    weights = (stacked, weight_p, weight_2, weight_m)
    blocks0 = (own0, minus0, plus0, far0, own0_s, minus0_s, plus0_s, far0_s)
    returned, plain, all0 = return_blocks(0, weights, blocks0)
    columns, flipped = gather_columns(after(quarters[0], returned), *quarters[1:])
    minus1, far1, columns, flipped = lax.optimization_barrier((minus1, far1, columns, flipped))

    minus1_s, far1_s = swap(minus1), swap(far1)
    blocks1 = (own1, minus1, plus1, far1, own1_s, minus1_s, plus1_s, far1_s)
    returned, gain_part, all1 = return_blocks(1, weights, blocks1, columns, plain, returned)
    layers = exchange(returned, SEC)
    query_in = lax.ppermute(
        after(local, minus1_s, far1_s), SEC, [(s, s - 1) for s in range(1, 8)]
    )
    gains = [gain_part] + [shift(gain_part, "x", r) for r in (1, 2, 3)]
    part = weight_blocks(after(flipped, returned), all0, all1)
    sums = sum_layers(after(layers, part[0]), gains)
    own = exchange(sums, ZC)
    far_p, far_m = lax.optimization_barrier((part[3], part[4], *gains))[:2]
    far_p, far_m = shift(far_p, "x", 1), shift(far_m, "x", -1)
    near_p, near_m = relay_blocks(part[1], part[2], far_p, far_m)
    packed = encoder_rows(after(own, near_p, query_in), hidden, gain)
    near_p, near_m = shift(near_p, "x", 1), shift(near_m, "x", -1)
    other = lax.ppermute(packed, "zlo", [(0, 1), (1, 0)])
    packed = jnp.stack([packed, other])
    packed = [packed] + [shift(packed, "y", -r) for r in (1, 2, 3)]
    grad_key, grad_value = add_blocks(part[0], near_p, near_m)
    query_grad = hand_on(query_in)
    encoder_grad, gain_grad = finish(packed, gain)
    return (
        query_grad,
        grad_key[None],
        grad_value[None],
        encoder_grad.reshape(pre_norm.shape),
        gain_grad.reshape(features),
    )


def solution(mesh):
    grid = Mesh(mesh.devices.reshape(4, 2, 4, 4, 2), ("y", "zlo", "zhi", "x", "core"))
    dp = ("zhi", "x", "core")
    return jax.shard_map(
        body,
        mesh=grid,
        in_specs=(
            P(None, dp, None, None),
            P(),
            P(SEC, None, dp, None, None),
            P(SEC, None, dp, None, None),
            P(SEC, None, dp, None, None),
            P(SEC, None, dp, None, None),
            P(SEC, dp, None),
            P(SEC, dp, None),
        ),
        out_specs=(
            P(SEC, None, dp, None, None),
            P(SEC, dp, None),
            P(SEC, dp, None),
            P(None, dp, None, None),
            P(),
        ),
        check_vma=False,
    )
```

```python
import functools

import jax
import jax.numpy as jnp
from jax import lax
from jax.experimental import pallas as pl
from jax.experimental.pallas import tpu as pltpu
from jax.sharding import Mesh, PartitionSpec as P

EPS = 1e-06
BF = jnp.bfloat16
F32 = jnp.float32
SEC = ("y", "zlo")
ZC = ("zhi", "core")
SRC = 48
D = 4096
HD = 2048
COLS = 512
PIECE = 6
VMEM = pl.BlockSpec(memory_space=pltpu.VMEM)
HBM = pl.BlockSpec(memory_space=pl.ANY)
PIN = pl.BlockSpec(memory_space=pltpu.HBM)


def shape(dims, dtype=BF):
    return jax.ShapeDtypeStruct(dims, dtype)


def pinned(dims, dtype=BF):
    return pltpu.HBM(dims, dtype)


def hold(*values):
    return [pltpu.with_memory_space_constraint(v, pltpu.HBM) for v in values]


def params(mib=16):
    return pltpu.CompilerParams(vmem_limit_bytes=mib * 2**20)


def cost(megabytes=0):
    return pl.CostEstimate(flops=0, bytes_accessed=megabytes * 2**20, transcendentals=0)


def rows_dot(a, b):
    return lax.dot_general(a, b, (((1,), (1,)), ((), ())), preferred_element_type=F32)


def columns_dot(a, b):
    return lax.dot_general(a, b, (((0,), (0,)), ((), ())), preferred_element_type=F32)


def heads_kernel(first, q_ref, k_ref, v_ref, g_ref, *refs):
    if first:
        key_w, value_w, local_ref, grads_ref, stack_ref = refs
        stack_ref[0], stack_ref[1] = key_w[0], value_w[0]
    else:
        _, local_ref, grads_ref = refs
    key_out = grads_ref.at[:, pl.ds(0, HD)]
    value_out = grads_ref.at[:, pl.ds(HD, HD)]
    src = k_ref.shape[0]
    lane = lax.broadcasted_iota(jnp.int32, (src, 256), 1) // 64
    masks = [lane == h for h in range(4)]

    def spread(block):
        zero = jnp.zeros_like(block)
        return jnp.concatenate([jnp.where(m, block, zero) for m in masks], axis=0)

    def diagonal(wide):
        out = wide[:src]
        for h in range(1, 4):
            out = jnp.where(masks[h], wide[h * src : (h + 1) * src], out)
        return out

    for part in range(HD // 256):
        at = pl.ds(part * 256, 256)
        q, g = q_ref[:, at], g_ref[:, at]
        k, v = spread(k_ref[:, at]), spread(v_ref[:, at])
        scores = rows_dot(k, q).reshape(4, src, -1)
        exponent = jnp.exp(scores - jnp.max(scores, axis=1, keepdims=True))
        probs = exponent * (1.0 / jnp.sum(exponent, axis=1, keepdims=True))
        slopes = rows_dot(v, g).reshape(4, src, -1)
        center = jnp.sum(probs * slopes, axis=1, keepdims=True)
        score_grad = (probs * (slopes - center)).astype(BF).reshape(4 * src, -1)
        probs = probs.astype(BF).reshape(4 * src, -1)
        value = jnp.dot(probs, g, preferred_element_type=F32)
        key = jnp.dot(score_grad, q, preferred_element_type=F32)
        key_out[:, at] = diagonal(key).astype(BF)
        value_out[:, at] = diagonal(value).astype(BF)
        local_ref[:, at] = columns_dot(score_grad, k).astype(BF)


def heads(q, k, v, g, m, *others):
    tgt = q.shape[3]

    def row(n):
        return pl.BlockSpec((None, None, None, n, HD), lambda i: (0, m, 0, 0, 0))

    def whole(*dims):
        return pl.BlockSpec(dims, lambda i: (0,) * len(dims))

    if m == 0:
        outs, more = [(SRC, D), (2, 128, HD)], [whole(1, 128, HD)] * 2
    else:
        outs, more = [(SRC, D)], [HBM]
    return pl.pallas_call(
        functools.partial(heads_kernel, m == 0),
        grid=(1,),
        in_specs=[row(tgt), row(SRC), row(SRC), row(tgt)] + more,
        out_specs=[row(tgt)] + [whole(*dims) for dims in outs],
        out_shape=[shape(q.shape)] + [shape(dims) for dims in outs],
        input_output_aliases={} if m == 0 else {4: 0},
        compiler_params=params(60),
        cost_estimate=cost(40),
        name="heads",
    )(q, k, v, g, *others)


def memory_kernel(pre_ref, gain_ref, out_ref):
    rows, features = pre_ref.shape
    squares = jnp.zeros((rows, 128), F32)
    for n in range(features // 128):
        part = pre_ref[:, pl.ds(n * 128, 128)].astype(F32)
        squares += part * part
    inverse = lax.rsqrt(jnp.sum(squares, axis=-1, keepdims=True) / features + EPS)
    for z in range(4):
        for c in range(2):
            at = pl.ds(pl.multiple_of(((z * 4 + lax.axis_index("y")) * 2 + c) * 128, 128), 128)
            hidden = pre_ref[:, at].astype(F32)
            out_ref[z * 2 + c] = (hidden * inverse * gain_ref[:, at]).astype(BF)


def memory_blocks(pre, gain):
    rows = pre.shape[0]
    return pl.pallas_call(
        memory_kernel,
        in_specs=[VMEM, VMEM],
        out_specs=VMEM,
        out_shape=shape((8, rows, 128)),
        compiler_params=params(60),
        cost_estimate=cost(),
        name="memory",
    )(pre, gain)


def token_blocks():
    z, c = lax.axis_index("zhi"), lax.axis_index("core")
    index = []
    for core in (c, 1 - c):
        for step in (0, 3, 1, 2):
            index.append(lax.rem(z + step, 4) * 2 + core)
    return index


def start_all(pairs, sems, first=0):
    copies = [pltpu.make_async_copy(a, b, sems.at[first + i]) for i, (a, b) in enumerate(pairs)]
    for copy in copies:
        copy.start()
    return copies


def wait_all(copies):
    for copy in copies:
        copy.wait()


def lanes(index):
    return pl.ds(pl.multiple_of(index * 128, 128), 128)


def columns_kernel(*refs):
    cols, out_ref, flip_ref, cols_s, flip_s, sems = refs[:4], *refs[4:]
    x, y = lax.axis_index("x"), lax.axis_index("y")
    pairs = []
    for r in range(4):
        at = lanes(lax.rem(y + r + 4 - x, 4))
        for m in range(2):
            pairs.append((cols[r].at[:, m], cols_s.at[m, :, :, at]))
    wait_all(start_all(pairs, sems))
    columns = cols_s[...].reshape(16 * SRC, COLS)
    kept = start_all([(cols_s, out_ref)], sems)
    for n in range(6):
        at = slice(n * 128, (n + 1) * 128)
        flip_s[:, at] = columns[at].T
    wait_all(kept + start_all([(flip_s, flip_ref)], sems, 1))


def gather_columns(*columns):
    return pl.pallas_call(
        columns_kernel,
        in_specs=[HBM] * 4,
        out_specs=[PIN, PIN],
        out_shape=[pinned((2, 8, SRC, COLS)), pinned((COLS, 16 * SRC))],
        scratch_shapes=[
            pltpu.VMEM((2, 8, SRC, COLS), BF),
            pltpu.VMEM((COLS, 16 * SRC), BF),
            pltpu.SemaphoreType.DMA((8,)),
        ],
        compiler_params=params(),
        cost_estimate=cost(),
        name="columns",
    )(*columns)


def return_kernel(m, *refs):
    weights, grads, refs = refs[:4], refs[4:12], refs[12:]
    if m == 0:
        out_ref, plain_ref, all_ref, grad_s, weight_s, out_s, plain_s, sems = refs
    else:
        cols_ref, before_ref, _, out_ref, gain_ref, all_ref = refs[:6]
        grad_s, weight_s, out_s, plain_s, cols_s, sems = refs[6:]
    x = lax.axis_index("x")
    place = token_blocks()
    pairs = []
    for half in range(2):
        for i, ref in enumerate(grads):
            pairs.append((ref.at[:, pl.ds(half * HD, HD)], grad_s.at[half, place[i]]))
        for r, ref in enumerate(weights):
            pairs.append((ref.at[half], weight_s.at[half, pl.ds(r * 128, 128)]))
    if m == 1:
        pairs += [(cols_ref, cols_s), (before_ref, plain_s)]
    copies = start_all(pairs, sems)
    wait_all(copies[:12])
    result = rows_dot(grad_s[0].reshape(8 * SRC, HD), weight_s[0])
    wait_all(copies[12:])
    kept = start_all([(grad_s, all_ref)], sems)
    result += rows_dot(grad_s[1].reshape(8 * SRC, HD), weight_s[1])
    rounded = result.astype(BF)
    if m == 0:
        plain_s[...] = rounded
        kept += start_all([(plain_s, plain_ref)], sems, 1)
    else:
        first, second = (cols_s[i].reshape(8 * SRC, COLS).astype(F32) for i in range(2))
        gain = jnp.sum(plain_s[...].astype(F32) * first + result * second, axis=0, keepdims=True)
        for r in range(4):
            block = gain[:, r * 128 : (r + 1) * 128]
            gain_ref[:, lanes(lax.rem(x + r, 4))] = jnp.broadcast_to(block, (8, 128))
    rows = 8 * SRC
    target = lax.broadcasted_iota(jnp.int32, (rows, rows), 0)
    source = lax.broadcasted_iota(jnp.int32, (rows, rows), 1)
    rank, rest = target // SRC, target % SRC
    wanted = (rest // PIECE) * SRC + rank * PIECE + rest % PIECE
    move = (source == wanted).astype(F32).astype(BF)
    moved = jnp.dot(move, rounded, preferred_element_type=F32)
    out_s[...] = moved.astype(BF).reshape(8, SRC, COLS)
    wait_all(kept + start_all([(out_s, out_ref.at[:, m])], sems, 2))


def return_blocks(m, weights, grads, *more):
    outs = [pinned((8, 2, SRC, COLS)), pinned((8 * SRC, COLS)), pinned((2, 8, SRC, HD))]
    scratch = [
        pltpu.VMEM((2, 8, SRC, HD), BF),
        pltpu.VMEM((2, COLS, HD), BF),
        pltpu.VMEM((8, SRC, COLS), BF),
        pltpu.VMEM((8 * SRC, COLS), BF),
    ]
    if m == 1:
        outs[1] = shape((8, COLS), F32)
        scratch.append(pltpu.VMEM((2, 8, SRC, COLS), BF))
    return pl.pallas_call(
        functools.partial(return_kernel, m),
        in_specs=[HBM] * 12 + [PIN] * len(more),
        out_specs=[PIN, VMEM if m == 1 else PIN, PIN],
        out_shape=outs,
        input_output_aliases={14: 0} if m == 1 else {},
        scratch_shapes=scratch + [pltpu.SemaphoreType.DMA((26,))],
        compiler_params=params(),
        cost_estimate=cost(),
        name="returned",
    )(*weights, *grads, *hold(*more))


def weight_kernel(flip_ref, first_ref, second_ref, *refs):
    own, sum_p, sum_m, raw_p, raw_m, far_p, far_m, grad_s, flip_s, own_s, sum_s, sems = refs
    kept = []
    pairs = [(flip_ref, flip_s)]
    for half in (1, 0):
        for m, ref in enumerate((first_ref, second_ref)):
            pairs.append((ref.at[half], grad_s.at[half, m]))
    copies = start_all(pairs, sems)
    for half in (1, 0):
        wait_all(copies[:3] if half == 1 else copies[3:])
        for n in range(HD // 512):
            at = pl.ds(n * 512, 512)
            grad = grad_s[half, :, :, :, at].reshape(16 * SRC, 512)
            partial = jnp.dot(flip_s[...], grad, preferred_element_type=F32).astype(BF)
            own_s[half, :, at] = partial[:128]
            sum_s[0, half, :, at] = partial[128:192]
            raw_p[half, :, at] = partial[192:256]
            far_p[half, :, at] = partial[256:320]
            far_m[half, :, at] = partial[320:384]
            raw_m[half, :, at] = partial[384:448]
            sum_s[1, half, :, at] = partial[448:]
        pairs = [(own_s.at[half], own.at[half])]
        pairs += [(sum_s.at[i, half], out.at[half]) for i, out in enumerate((sum_p, sum_m))]
        kept += start_all(pairs, sems, 5 + 3 * half)
    wait_all(kept)


def weight_blocks(flipped, first, second):
    return pl.pallas_call(
        weight_kernel,
        in_specs=[PIN] * 3,
        out_specs=[PIN] * 3 + [VMEM] * 4,
        out_shape=[pinned((2, n, HD)) for n in (128, 64, 64)] + [shape((2, 64, HD))] * 4,
        scratch_shapes=[
            pltpu.VMEM((2, 2, 8, SRC, HD), BF),
            pltpu.VMEM((COLS, 16 * SRC), BF),
            pltpu.VMEM((2, 128, HD), BF),
            pltpu.VMEM((2, 2, 64, HD), BF),
            pltpu.SemaphoreType.DMA((11,)),
        ],
        compiler_params=params(),
        cost_estimate=cost(),
        name="weights",
    )(*hold(flipped, first, second))


def relay_kernel(sum_p, sum_m, far_p, far_m, out_p, out_m, terms_s, sems):
    refs = (sum_p, sum_m, far_p, far_m)
    wait_all(start_all([(ref, terms_s.at[i]) for i, ref in enumerate(refs)], sems))
    out_p[...] = (terms_s[0].astype(F32) + terms_s[2].astype(F32)).astype(BF)
    out_m[...] = (terms_s[1].astype(F32) + terms_s[3].astype(F32)).astype(BF)


def relay_blocks(sum_p, sum_m, far_p, far_m):
    return pl.pallas_call(
        relay_kernel,
        in_specs=[PIN, PIN, HBM, HBM],
        out_specs=[VMEM] * 2,
        out_shape=[shape(sum_p.shape)] * 2,
        scratch_shapes=[pltpu.VMEM((4, 2, 64, HD), BF), pltpu.SemaphoreType.DMA((4,))],
        compiler_params=params(),
        cost_estimate=cost(),
        name="relay",
    )(*hold(sum_p, sum_m), far_p, far_m)


def pick_rows(rows, cols, wanted, keep):
    target = lax.broadcasted_iota(jnp.int32, (rows, cols), 0)
    source = lax.broadcasted_iota(jnp.int32, (rows, cols), 1)
    return ((source == wanted(target)) & keep(target)).astype(F32).astype(BF)


def sum_kernel(layers_ref, gain0_ref, gain1_ref, gain2_ref, gain3_ref, out_ref):
    moved = jnp.zeros((128, COLS), F32)
    for m in range(2):
        total = jnp.sum(layers_ref[:, m].astype(F32), axis=0).astype(BF)
        move = pick_rows(
            128,
            SRC,
            lambda t: (t // 16) * PIECE + t % 16 - m * PIECE,
            lambda t: (t % 16 >= m * PIECE) & (t % 16 < (m + 1) * PIECE),
        )
        moved += jnp.dot(move, total, preferred_element_type=F32)
    blocks = [lanes(lax.rem(lax.axis_index("x") + r, 4)) for r in range(4)]
    gains = (gain0_ref, gain1_ref, gain2_ref, gain3_ref)
    gain = jnp.concatenate([sum(ref[:, at] for ref in gains)[:1] for at in blocks], axis=1)
    high = gain.astype(BF).astype(F32)
    row = lax.broadcasted_iota(jnp.int32, (128, COLS), 0) % 16
    moved = jnp.where(row == 12, high, jnp.where(row == 13, gain - high, moved))
    out_ref[...] = moved.astype(BF).reshape(8, 16, COLS)


def sum_layers(layers, gains):
    return pl.pallas_call(
        sum_kernel,
        in_specs=[VMEM] * 5,
        out_specs=VMEM,
        out_shape=shape((8, 16, COLS)),
        compiler_params=params(),
        cost_estimate=cost(),
        name="layers",
    )(layers, *gains)


def encoder_kernel(
    own_ref, pre_ref, gain_ref, out_ref, full_s
):
    for z in range(4):
        for c in range(2):
            for x in range(4):
                at = (z * 4 + lax.rem(lax.axis_index("x") + x, 4)) * 2 + c
                full_s[:, lanes(at)] = own_ref[z * 2 + c, :, x * 128 : (x + 1) * 128]
    own = full_s[...].astype(F32)
    rank = (lax.axis_index("y") * 2 + lax.axis_index("zlo"))
    pick = pick_rows(
        16,
        2 * SRC,
        lambda t: (t // PIECE) * SRC + rank * PIECE + t % PIECE,
        lambda t: t < 2 * PIECE,
    )
    hidden = jnp.dot(pick, pre_ref[...], preferred_element_type=F32)
    inverse = lax.rsqrt(jnp.mean(hidden * hidden, axis=-1, keepdims=True) + EPS)
    scaled = own * gain_ref[...]
    row_mean = jnp.mean(hidden * scaled, axis=-1, keepdims=True)
    mine = inverse * scaled - hidden * (inverse * inverse * inverse * row_mean)
    row = lax.broadcasted_iota(jnp.int32, (16, D), 0)
    packed = jnp.where(row < 2 * PIECE, mine, own).astype(BF)
    out_ref[...] = packed


def encoder_rows(own, pre, gain):
    return pl.pallas_call(
        encoder_kernel,
        in_specs=[VMEM, VMEM, VMEM],
        out_specs=VMEM,
        out_shape=shape((16, D)),
        scratch_shapes=[pltpu.VMEM((16, D), BF)],
        compiler_params=params(),
        cost_estimate=cost(),
        name="encoder",
    )(own, pre, gain)


def finish_kernel(a_ref, b_ref, c_ref, d_ref, gain_ref, out_ref, gain_out_ref, packed_s):
    y, zlo = lax.axis_index("y"), lax.axis_index("zlo")
    for r, ref in enumerate((a_ref, b_ref, c_ref, d_ref)):
        for j in range(2):
            rank = lax.rem(y + r, 4) * 2 + (zlo if j == 0 else 1 - zlo)
            packed_s[rank] = ref[j]
    packed = packed_s[...].reshape(128, D)
    move = pick_rows(
        2 * SRC,
        128,
        lambda t: ((t % SRC) // PIECE) * 16 + (t // SRC) * PIECE + t % PIECE,
        lambda t: t >= 0,
    )
    out_ref[...] = jnp.dot(move, packed, preferred_element_type=F32).astype(BF)
    target = lax.broadcasted_iota(jnp.int32, (16, 128), 1) % 16
    ones = ((target == 12) | (target == 13)).astype(F32).astype(BF)
    gain = jnp.dot(ones, packed, preferred_element_type=F32)
    gain_out_ref[...] = gain[:1] / gain_ref[...]


def finish(packed, gain):
    return pl.pallas_call(
        finish_kernel,
        in_specs=[VMEM] * 5,
        out_specs=[VMEM, VMEM],
        out_shape=[shape((2 * SRC, D)), shape((1, D), F32)],
        scratch_shapes=[pltpu.VMEM((8, 16, D), BF)],
        compiler_params=params(),
        cost_estimate=cost(),
        name="finish",
    )(*packed, gain)


def add_kernel(own_ref, *refs):
    terms, (key_out, value_out), (own_s, terms_s, sems) = refs[:4], refs[4:6], refs[6:]
    copies = start_all([(own_ref, own_s)], sems)
    wait_all(copies + start_all([(ref, terms_s.at[i]) for i, ref in enumerate(terms)], sems, 1))
    for half, out in enumerate((key_out, value_out)):
        for rows, first, second in ((0, 0, 3), (64, 2, 1)):
            total = own_s[half, rows : rows + 64].astype(F32) + terms_s[first, half].astype(F32)
            out[rows : rows + 64] = (total + terms_s[second, half].astype(F32)).astype(BF)


def add_blocks(own, *terms):
    dims = own.shape
    return pl.pallas_call(
        add_kernel,
        in_specs=[PIN] + [HBM] * 4,
        out_specs=[VMEM] * 2,
        out_shape=[shape(dims[1:])] * 2,
        scratch_shapes=[
            pltpu.VMEM(dims, BF),
            pltpu.VMEM((4,) + terms[0].shape, BF),
            pltpu.SemaphoreType.DMA((5,)),
        ],
        compiler_params=params(),
        cost_estimate=cost(),
        name="add",
    )(*hold(own), *terms)


def hand_kernel(in_ref, out_ref, held_s, sems):
    wait_all(start_all([(in_ref, held_s)], sems))
    wait_all(start_all([(held_s, out_ref)], sems))


def hand_on(value):
    return pl.pallas_call(
        hand_kernel,
        in_specs=[HBM],
        out_specs=PIN,
        out_shape=pinned(value.shape),
        scratch_shapes=[pltpu.VMEM(value.shape, BF), pltpu.SemaphoreType.DMA((1,))],
        compiler_params=params(),
        cost_estimate=cost(400),
        name="hand",
    )(value)


def shift(value, axis, step):
    return lax.ppermute(value, axis, [(i, (i + step) % 4) for i in range(4)])


def swap(value):
    return lax.ppermute(value, "core", [(0, 1), (1, 0)])


def after(value, *others):
    return lax.optimization_barrier((value,) + others)[0]


def exchange(value, axes):
    return lax.all_to_all(value, axes, split_axis=0, concat_axis=0, tiled=True)


def body(pre_norm, norm_gain, queries, keys, values, head_grad, key_weight, value_weight):
    batches, _, source_n, features = pre_norm.shape
    rows = batches * source_n
    gain = norm_gain.reshape(1, features)
    hidden = pre_norm.reshape(rows, features)

    local, own0, stacked = heads(queries, keys, values, head_grad, 0, key_weight, value_weight)
    minus0, plus0 = shift(own0, "zhi", 1), shift(own0, "zhi", -1)
    own0_s = swap(own0)
    weight_m, weight_p = shift(stacked, "x", 1), shift(stacked, "x", -1)
    blocks = memory_blocks(after(hidden, own0), gain)
    quarter = exchange(blocks, ZC).reshape(8, batches, source_n, 128)
    local, own1 = heads(after(queries, blocks), keys, values, head_grad, 1, local)
    minus0, plus0, weight_m, weight_p, own1, own0_s, quarter = lax.optimization_barrier(
        (minus0, plus0, weight_m, weight_p, own1, own0_s, quarter)
    )

    far0 = shift(minus0, "zhi", 1)
    plus1 = shift(own1, "zhi", -1)
    weight_2 = shift(after(stacked, weight_m), "x", 2)
    minus0_s, plus0_s, own1_s = swap(minus0), swap(plus0), swap(own1)
    far0, plus1, quarter = lax.optimization_barrier((far0, plus1, quarter))

    minus1 = shift(after(own1, far0), "zhi", 1)
    far1 = shift(plus1, "zhi", -1)
    far0_s, plus1_s = swap(far0), swap(plus1)
    quarters = [quarter] + [shift(quarter, "y", -r) for r in (1, 2, 3)]
    weights = (stacked, weight_p, weight_2, weight_m)
    blocks0 = (own0, minus0, plus0, far0, own0_s, minus0_s, plus0_s, far0_s)
    returned, plain, all0 = return_blocks(0, weights, blocks0)
    columns, flipped = gather_columns(after(quarters[0], returned), *quarters[1:])
    minus1, far1, columns, flipped = lax.optimization_barrier((minus1, far1, columns, flipped))

    minus1_s, far1_s = swap(minus1), swap(far1)
    blocks1 = (own1, minus1, plus1, far1, own1_s, minus1_s, plus1_s, far1_s)
    returned, gain_part, all1 = return_blocks(1, weights, blocks1, columns, plain, returned)
    layers = exchange(returned, SEC)
    query_in = lax.ppermute(
        after(local, minus1_s, far1_s), SEC, [(s, s - 1) for s in range(1, 8)]
    )
    gains = [gain_part] + [shift(gain_part, "x", r) for r in (1, 2, 3)]
    part = weight_blocks(after(flipped, returned), all0, all1)
    sums = sum_layers(after(layers, part[0]), gains)
    own = exchange(sums, ZC)
    own_part, sum_p, sum_m, raw_p, raw_m, far_p, far_m = part
    far_p, far_m, raw_p, raw_m = lax.optimization_barrier((far_p, far_m, raw_p, raw_m, *gains))[:4]
    far_p, far_m = shift(far_p, "x", 1), shift(far_m, "x", -1)
    raw_p, raw_m = shift(raw_p, "x", 1), shift(raw_m, "x", -1)
    far_p, far_m = lax.optimization_barrier((far_p, far_m, raw_p, raw_m))[:2]
    sum_p, sum_m = relay_blocks(sum_p, sum_m, far_p, far_m)
    packed = encoder_rows(after(own, query_in), hidden, gain)
    sum_p, sum_m = shift(sum_p, "x", 1), shift(sum_m, "x", -1)
    other = lax.ppermute(packed, "zlo", [(0, 1), (1, 0)])
    packed = jnp.stack([packed, other])
    packed = [packed] + [shift(packed, "y", -r) for r in (1, 2, 3)]
    grad_key, grad_value = add_blocks(own_part, sum_p, sum_m, raw_p, raw_m)
    query_grad = hand_on(query_in)
    encoder_grad, gain_grad = finish(packed, gain)
    return (
        query_grad,
        grad_key[None],
        grad_value[None],
        encoder_grad.reshape(pre_norm.shape),
        gain_grad.reshape(features),
    )


def solution(mesh):
    grid = Mesh(mesh.devices.reshape(4, 2, 4, 4, 2), ("y", "zlo", "zhi", "x", "core"))
    dp = ("zhi", "x", "core")
    return jax.shard_map(
        body,
        mesh=grid,
        in_specs=(
            P(None, dp, None, None),
            P(),
            P(SEC, None, dp, None, None),
            P(SEC, None, dp, None, None),
            P(SEC, None, dp, None, None),
            P(SEC, None, dp, None, None),
            P(SEC, dp, None),
            P(SEC, dp, None),
        ),
        out_specs=(
            P(SEC, None, dp, None, None),
            P(SEC, dp, None),
            P(SEC, dp, None),
            P(None, dp, None, None),
            P(),
        ),
        check_vma=False,
    )
```

```python
import functools

import jax
import jax.numpy as jnp
from jax import lax
from jax.experimental import pallas as pl
from jax.experimental.pallas import tpu as pltpu
from jax.sharding import Mesh, PartitionSpec as P

EPS = 1e-06
BF = jnp.bfloat16
F32 = jnp.float32
SEC = ("y", "zlo")
ZC = ("zhi", "core")
SRC = 48
D = 4096
HD = 2048
COLS = 512
PIECE = 6
VMEM = pl.BlockSpec(memory_space=pltpu.VMEM)
HBM = pl.BlockSpec(memory_space=pl.ANY)
PIN = pl.BlockSpec(memory_space=pltpu.HBM)


def shape(dims, dtype=BF):
    return jax.ShapeDtypeStruct(dims, dtype)


def pinned(dims, dtype=BF):
    return pltpu.HBM(dims, dtype)


def hold(*values):
    return [pltpu.with_memory_space_constraint(v, pltpu.HBM) for v in values]


def params(mib=16):
    return pltpu.CompilerParams(vmem_limit_bytes=mib * 2**20)


def cost(megabytes=0):
    return pl.CostEstimate(flops=0, bytes_accessed=megabytes * 2**20, transcendentals=0)


def rows_dot(a, b):
    return lax.dot_general(a, b, (((1,), (1,)), ((), ())), preferred_element_type=F32)


def columns_dot(a, b):
    return lax.dot_general(a, b, (((0,), (0,)), ((), ())), preferred_element_type=F32)


def heads_kernel(first, q_ref, k_ref, v_ref, g_ref, *refs):
    if first:
        key_w, value_w, local_ref, grads_ref, stack_ref = refs
        stack_ref[0], stack_ref[1] = key_w[0], value_w[0]
    else:
        _, local_ref, grads_ref = refs
    key_out = grads_ref.at[:, pl.ds(0, HD)]
    value_out = grads_ref.at[:, pl.ds(HD, HD)]
    src = k_ref.shape[0]
    lane = lax.broadcasted_iota(jnp.int32, (src, 256), 1) // 64
    masks = [lane == h for h in range(4)]

    def spread(block):
        zero = jnp.zeros_like(block)
        return jnp.concatenate([jnp.where(m, block, zero) for m in masks], axis=0)

    def diagonal(wide):
        out = wide[:src]
        for h in range(1, 4):
            out = jnp.where(masks[h], wide[h * src : (h + 1) * src], out)
        return out

    for part in range(HD // 256):
        at = pl.ds(part * 256, 256)
        q, g = q_ref[:, at], g_ref[:, at]
        k, v = spread(k_ref[:, at]), spread(v_ref[:, at])
        scores = rows_dot(k, q).reshape(4, src, -1)
        exponent = jnp.exp(scores - jnp.max(scores, axis=1, keepdims=True))
        probs = exponent * (1.0 / jnp.sum(exponent, axis=1, keepdims=True))
        slopes = rows_dot(v, g).reshape(4, src, -1)
        center = jnp.sum(probs * slopes, axis=1, keepdims=True)
        score_grad = (probs * (slopes - center)).astype(BF).reshape(4 * src, -1)
        probs = probs.astype(BF).reshape(4 * src, -1)
        value = jnp.dot(probs, g, preferred_element_type=F32)
        key = jnp.dot(score_grad, q, preferred_element_type=F32)
        key_out[:, at] = diagonal(key).astype(BF)
        value_out[:, at] = diagonal(value).astype(BF)
        local_ref[:, at] = columns_dot(score_grad, k).astype(BF)


def heads(q, k, v, g, m, *others):
    tgt = q.shape[3]

    def row(n):
        return pl.BlockSpec((None, None, None, n, HD), lambda i: (0, m, 0, 0, 0))

    def whole(*dims):
        return pl.BlockSpec(dims, lambda i: (0,) * len(dims))

    if m == 0:
        outs, more = [(SRC, D), (2, 128, HD)], [whole(1, 128, HD)] * 2
    else:
        outs, more = [(SRC, D)], [HBM]
    return pl.pallas_call(
        functools.partial(heads_kernel, m == 0),
        grid=(1,),
        in_specs=[row(tgt), row(SRC), row(SRC), row(tgt)] + more,
        out_specs=[row(tgt)] + [whole(*dims) for dims in outs],
        out_shape=[shape(q.shape)] + [shape(dims) for dims in outs],
        input_output_aliases={} if m == 0 else {4: 0},
        compiler_params=params(60),
        cost_estimate=cost(40),
        name="heads",
    )(q, k, v, g, *others)


def memory_kernel(pre_ref, gain_ref, out_ref):
    rows, features = pre_ref.shape
    squares = jnp.zeros((rows, 128), F32)
    for n in range(features // 128):
        part = pre_ref[:, pl.ds(n * 128, 128)].astype(F32)
        squares += part * part
    inverse = lax.rsqrt(jnp.sum(squares, axis=-1, keepdims=True) / features + EPS)
    for z in range(4):
        for c in range(2):
            at = pl.ds(pl.multiple_of(((z * 4 + lax.axis_index("y")) * 2 + c) * 128, 128), 128)
            hidden = pre_ref[:, at].astype(F32)
            out_ref[z * 2 + c] = (hidden * inverse * gain_ref[:, at]).astype(BF)


def memory_blocks(pre, gain):
    rows = pre.shape[0]
    return pl.pallas_call(
        memory_kernel,
        in_specs=[VMEM, VMEM],
        out_specs=VMEM,
        out_shape=shape((8, rows, 128)),
        compiler_params=params(60),
        cost_estimate=cost(),
        name="memory",
    )(pre, gain)


def token_blocks():
    z, c = lax.axis_index("zhi"), lax.axis_index("core")
    index = []
    for core in (c, 1 - c):
        for step in (0, 3, 1, 2):
            index.append(lax.rem(z + step, 4) * 2 + core)
    return index


def start_all(pairs, sems, first=0):
    copies = [pltpu.make_async_copy(a, b, sems.at[first + i]) for i, (a, b) in enumerate(pairs)]
    for copy in copies:
        copy.start()
    return copies


def wait_all(copies):
    for copy in copies:
        copy.wait()


def lanes(index):
    return pl.ds(pl.multiple_of(index * 128, 128), 128)


def columns_kernel(*refs):
    cols, out_ref, flip_ref, cols_s, flip_s, sems = refs[:4], *refs[4:]
    x, y = lax.axis_index("x"), lax.axis_index("y")
    pairs = []
    for r in range(4):
        at = lanes(lax.rem(y + r + 4 - x, 4))
        for m in range(2):
            pairs.append((cols[r].at[:, m], cols_s.at[m, :, :, at]))
    wait_all(start_all(pairs, sems))
    columns = cols_s[...].reshape(16 * SRC, COLS)
    kept = start_all([(cols_s, out_ref)], sems)
    for n in range(6):
        at = slice(n * 128, (n + 1) * 128)
        flip_s[:, at] = columns[at].T
    wait_all(kept + start_all([(flip_s, flip_ref)], sems, 1))


def gather_columns(*columns):
    return pl.pallas_call(
        columns_kernel,
        in_specs=[HBM] * 4,
        out_specs=[PIN, PIN],
        out_shape=[pinned((2, 8, SRC, COLS)), pinned((COLS, 16 * SRC))],
        scratch_shapes=[
            pltpu.VMEM((2, 8, SRC, COLS), BF),
            pltpu.VMEM((COLS, 16 * SRC), BF),
            pltpu.SemaphoreType.DMA((8,)),
        ],
        compiler_params=params(),
        cost_estimate=cost(),
        name="columns",
    )(*columns)


def return_kernel(m, *refs):
    weights, grads, refs = refs[:4], refs[4:12], refs[12:]
    if m == 0:
        out_ref, plain_ref, all_ref, grad_s, weight_s, out_s, plain_s, sems = refs
    else:
        cols_ref, before_ref, _, out_ref, gain_ref, all_ref = refs[:6]
        grad_s, weight_s, out_s, plain_s, cols_s, sems = refs[6:]
    x = lax.axis_index("x")
    place = token_blocks()
    pairs = []
    for half in range(2):
        for i, ref in enumerate(grads):
            pairs.append((ref.at[:, pl.ds(half * HD, HD)], grad_s.at[half, place[i]]))
        for r, ref in enumerate(weights):
            pairs.append((ref.at[half], weight_s.at[half, pl.ds(r * 128, 128)]))
    if m == 1:
        pairs += [(cols_ref, cols_s), (before_ref, plain_s)]
    copies = start_all(pairs, sems)
    wait_all(copies[:12])
    result = rows_dot(grad_s[0].reshape(8 * SRC, HD), weight_s[0])
    wait_all(copies[12:])
    kept = start_all([(grad_s, all_ref)], sems)
    result += rows_dot(grad_s[1].reshape(8 * SRC, HD), weight_s[1])
    rounded = result.astype(BF)
    if m == 0:
        plain_s[...] = rounded
        kept += start_all([(plain_s, plain_ref)], sems, 1)
    else:
        first, second = (cols_s[i].reshape(8 * SRC, COLS).astype(F32) for i in range(2))
        gain = jnp.sum(plain_s[...].astype(F32) * first + result * second, axis=0, keepdims=True)
        for r in range(4):
            block = gain[:, r * 128 : (r + 1) * 128]
            gain_ref[:, lanes(lax.rem(x + r, 4))] = jnp.broadcast_to(block, (8, 128))
    rows = 8 * SRC
    target = lax.broadcasted_iota(jnp.int32, (rows, rows), 0)
    source = lax.broadcasted_iota(jnp.int32, (rows, rows), 1)
    rank, rest = target // SRC, target % SRC
    wanted = (rest // PIECE) * SRC + rank * PIECE + rest % PIECE
    move = (source == wanted).astype(F32).astype(BF)
    moved = jnp.dot(move, rounded, preferred_element_type=F32)
    out_s[...] = moved.astype(BF).reshape(8, SRC, COLS)
    wait_all(kept + start_all([(out_s, out_ref.at[:, m])], sems, 2))


def return_blocks(m, weights, grads, *more):
    outs = [pinned((8, 2, SRC, COLS)), pinned((8 * SRC, COLS)), pinned((2, 8, SRC, HD))]
    scratch = [
        pltpu.VMEM((2, 8, SRC, HD), BF),
        pltpu.VMEM((2, COLS, HD), BF),
        pltpu.VMEM((8, SRC, COLS), BF),
        pltpu.VMEM((8 * SRC, COLS), BF),
    ]
    if m == 1:
        outs[1] = shape((8, COLS), F32)
        scratch.append(pltpu.VMEM((2, 8, SRC, COLS), BF))
    return pl.pallas_call(
        functools.partial(return_kernel, m),
        in_specs=[HBM] * 12 + [PIN] * len(more),
        out_specs=[PIN, VMEM if m == 1 else PIN, PIN],
        out_shape=outs,
        input_output_aliases={14: 0} if m == 1 else {},
        scratch_shapes=scratch + [pltpu.SemaphoreType.DMA((26,))],
        compiler_params=params(),
        cost_estimate=cost(),
        name="returned",
    )(*weights, *grads, *hold(*more))


def weight_kernel(flip_ref, first_ref, second_ref, *refs):
    own, sum_p, sum_m, raw_p, raw_m, far_p, far_m, grad_s, flip_s, own_s, sum_s, sems = refs
    kept = []
    pairs = [(flip_ref, flip_s)]
    for half in (1, 0):
        for m, ref in enumerate((first_ref, second_ref)):
            pairs.append((ref.at[half], grad_s.at[half, m]))
    copies = start_all(pairs, sems)
    for half in (1, 0):
        wait_all(copies[:3] if half == 1 else copies[3:])
        for n in range(HD // 512):
            at = pl.ds(n * 512, 512)
            grad = grad_s[half, :, :, :, at].reshape(16 * SRC, 512)
            partial = jnp.dot(flip_s[...], grad, preferred_element_type=F32).astype(BF)
            own_s[half, :, at] = partial[:128]
            sum_s[0, half, :, at] = partial[128:192]
            raw_p[half, :, at] = partial[192:256]
            far_p[half, :, at] = partial[256:320]
            far_m[half, :, at] = partial[320:384]
            raw_m[half, :, at] = partial[384:448]
            sum_s[1, half, :, at] = partial[448:]
        pairs = [(own_s.at[half], own.at[half])]
        pairs += [(sum_s.at[i, half], out.at[half]) for i, out in enumerate((sum_p, sum_m))]
        kept += start_all(pairs, sems, 5 + 3 * half)
    wait_all(kept)


def weight_blocks(flipped, first, second):
    return pl.pallas_call(
        weight_kernel,
        in_specs=[PIN] * 3,
        out_specs=[PIN] * 3 + [VMEM] * 4,
        out_shape=[pinned((2, n, HD)) for n in (128, 64, 64)] + [shape((2, 64, HD))] * 4,
        scratch_shapes=[
            pltpu.VMEM((2, 2, 8, SRC, HD), BF),
            pltpu.VMEM((COLS, 16 * SRC), BF),
            pltpu.VMEM((2, 128, HD), BF),
            pltpu.VMEM((2, 2, 64, HD), BF),
            pltpu.SemaphoreType.DMA((11,)),
        ],
        compiler_params=params(),
        cost_estimate=cost(),
        name="weights",
    )(*hold(flipped, first, second))


def relay_kernel(sum_p, sum_m, far_p, far_m, out_p, out_m, terms_s, sems):
    refs = (sum_p, sum_m, far_p, far_m)
    wait_all(start_all([(ref, terms_s.at[i]) for i, ref in enumerate(refs)], sems))
    out_p[...] = (terms_s[0].astype(F32) + terms_s[2].astype(F32)).astype(BF)
    out_m[...] = (terms_s[1].astype(F32) + terms_s[3].astype(F32)).astype(BF)


def relay_blocks(sum_p, sum_m, far_p, far_m):
    return pl.pallas_call(
        relay_kernel,
        in_specs=[PIN, PIN, HBM, HBM],
        out_specs=[VMEM] * 2,
        out_shape=[shape(sum_p.shape)] * 2,
        scratch_shapes=[pltpu.VMEM((4, 2, 64, HD), BF), pltpu.SemaphoreType.DMA((4,))],
        compiler_params=params(),
        cost_estimate=cost(),
        name="relay",
    )(*hold(sum_p, sum_m), far_p, far_m)


def pick_rows(rows, cols, wanted, keep):
    target = lax.broadcasted_iota(jnp.int32, (rows, cols), 0)
    source = lax.broadcasted_iota(jnp.int32, (rows, cols), 1)
    return ((source == wanted(target)) & keep(target)).astype(F32).astype(BF)


def sum_kernel(layers_ref, gain0_ref, gain1_ref, gain2_ref, gain3_ref, out_ref):
    moved = jnp.zeros((128, COLS), F32)
    for m in range(2):
        total = jnp.sum(layers_ref[:, m].astype(F32), axis=0).astype(BF)
        move = pick_rows(
            128,
            SRC,
            lambda t: (t // 16) * PIECE + t % 16 - m * PIECE,
            lambda t: (t % 16 >= m * PIECE) & (t % 16 < (m + 1) * PIECE),
        )
        moved += jnp.dot(move, total, preferred_element_type=F32)
    blocks = [lanes(lax.rem(lax.axis_index("x") + r, 4)) for r in range(4)]
    gains = (gain0_ref, gain1_ref, gain2_ref, gain3_ref)
    gain = jnp.concatenate([sum(ref[:, at] for ref in gains)[:1] for at in blocks], axis=1)
    high = gain.astype(BF).astype(F32)
    row = lax.broadcasted_iota(jnp.int32, (128, COLS), 0) % 16
    moved = jnp.where(row == 12, high, jnp.where(row == 13, gain - high, moved))
    out_ref[...] = moved.astype(BF).reshape(8, 16, COLS)


def sum_layers(layers, gains):
    return pl.pallas_call(
        sum_kernel,
        in_specs=[VMEM] * 5,
        out_specs=VMEM,
        out_shape=shape((8, 16, COLS)),
        compiler_params=params(),
        cost_estimate=cost(),
        name="layers",
    )(layers, *gains)


def encoder_kernel(
    own_ref, pre_ref, gain_ref, out_ref, full_s
):
    for z in range(4):
        for c in range(2):
            for x in range(4):
                at = (z * 4 + lax.rem(lax.axis_index("x") + x, 4)) * 2 + c
                full_s[:, lanes(at)] = own_ref[z * 2 + c, :, x * 128 : (x + 1) * 128]
    own = full_s[...].astype(F32)
    rank = (lax.axis_index("y") * 2 + lax.axis_index("zlo"))
    pick = pick_rows(
        16,
        2 * SRC,
        lambda t: (t // PIECE) * SRC + rank * PIECE + t % PIECE,
        lambda t: t < 2 * PIECE,
    )
    hidden = jnp.dot(pick, pre_ref[...], preferred_element_type=F32)
    inverse = lax.rsqrt(jnp.mean(hidden * hidden, axis=-1, keepdims=True) + EPS)
    scaled = own * gain_ref[...]
    row_mean = jnp.mean(hidden * scaled, axis=-1, keepdims=True)
    mine = inverse * scaled - hidden * (inverse * inverse * inverse * row_mean)
    row = lax.broadcasted_iota(jnp.int32, (16, D), 0)
    packed = jnp.where(row < 2 * PIECE, mine, own).astype(BF)
    out_ref[...] = packed


def encoder_rows(own, pre, gain):
    return pl.pallas_call(
        encoder_kernel,
        in_specs=[VMEM, VMEM, VMEM],
        out_specs=VMEM,
        out_shape=shape((16, D)),
        scratch_shapes=[pltpu.VMEM((16, D), BF)],
        compiler_params=params(),
        cost_estimate=cost(),
        name="encoder",
    )(own, pre, gain)


def finish_kernel(a_ref, b_ref, c_ref, d_ref, gain_ref, out_ref, gain_out_ref, packed_s):
    y, zlo = lax.axis_index("y"), lax.axis_index("zlo")
    for r, ref in enumerate((a_ref, b_ref, c_ref, d_ref)):
        for j in range(2):
            rank = lax.rem(y + r, 4) * 2 + (zlo if j == 0 else 1 - zlo)
            packed_s[rank] = ref[j]
    packed = packed_s[...].reshape(128, D)
    move = pick_rows(
        2 * SRC,
        128,
        lambda t: ((t % SRC) // PIECE) * 16 + (t // SRC) * PIECE + t % PIECE,
        lambda t: t >= 0,
    )
    out_ref[...] = jnp.dot(move, packed, preferred_element_type=F32).astype(BF)
    target = lax.broadcasted_iota(jnp.int32, (16, 128), 1) % 16
    ones = ((target == 12) | (target == 13)).astype(F32).astype(BF)
    gain = jnp.dot(ones, packed, preferred_element_type=F32)
    gain_out_ref[...] = gain[:1] / gain_ref[...]


def finish(packed, gain):
    return pl.pallas_call(
        finish_kernel,
        in_specs=[VMEM] * 5,
        out_specs=[VMEM, VMEM],
        out_shape=[shape((2 * SRC, D)), shape((1, D), F32)],
        scratch_shapes=[pltpu.VMEM((8, 16, D), BF)],
        compiler_params=params(),
        cost_estimate=cost(),
        name="finish",
    )(*packed, gain)


def add_kernel(own_ref, *refs):
    terms, (key_out, value_out), (own_s, terms_s, sems) = refs[:4], refs[4:6], refs[6:]
    copies = start_all([(own_ref, own_s)], sems)
    wait_all(copies + start_all([(ref, terms_s.at[i]) for i, ref in enumerate(terms)], sems, 1))
    for half, out in enumerate((key_out, value_out)):
        for rows, first, second in ((0, 0, 3), (64, 2, 1)):
            total = own_s[half, rows : rows + 64].astype(F32) + terms_s[first, half].astype(F32)
            out[rows : rows + 64] = (total + terms_s[second, half].astype(F32)).astype(BF)


def add_blocks(own, *terms):
    dims = own.shape
    return pl.pallas_call(
        add_kernel,
        in_specs=[PIN] + [HBM] * 4,
        out_specs=[VMEM] * 2,
        out_shape=[shape(dims[1:])] * 2,
        scratch_shapes=[
            pltpu.VMEM(dims, BF),
            pltpu.VMEM((4,) + terms[0].shape, BF),
            pltpu.SemaphoreType.DMA((5,)),
        ],
        compiler_params=params(),
        cost_estimate=cost(),
        name="add",
    )(*hold(own), *terms)


def hand_kernel(in_ref, out_ref, held_s, sems):
    wait_all(start_all([(in_ref, held_s)], sems))
    wait_all(start_all([(held_s, out_ref)], sems))


def hand_on(value):
    return pl.pallas_call(
        hand_kernel,
        in_specs=[HBM],
        out_specs=PIN,
        out_shape=pinned(value.shape),
        scratch_shapes=[pltpu.VMEM(value.shape, BF), pltpu.SemaphoreType.DMA((1,))],
        compiler_params=params(),
        cost_estimate=cost(400),
        name="hand",
    )(value)


def shift(value, axis, step):
    return lax.ppermute(value, axis, [(i, (i + step) % 4) for i in range(4)])


def swap(value):
    return lax.ppermute(value, "core", [(0, 1), (1, 0)])


def after(value, *others):
    return lax.optimization_barrier((value,) + others)[0]


def exchange(value, axes):
    return lax.all_to_all(value, axes, split_axis=0, concat_axis=0, tiled=True)


def body(pre_norm, norm_gain, queries, keys, values, head_grad, key_weight, value_weight):
    batches, _, source_n, features = pre_norm.shape
    rows = batches * source_n
    gain = norm_gain.reshape(1, features)
    hidden = pre_norm.reshape(rows, features)

    local, own0, stacked = heads(queries, keys, values, head_grad, 0, key_weight, value_weight)
    minus0, plus0 = shift(own0, "zhi", 1), shift(own0, "zhi", -1)
    own0_s = swap(own0)
    weight_m, weight_p = shift(stacked, "x", 1), shift(stacked, "x", -1)
    blocks = memory_blocks(after(hidden, own0), gain)
    quarter = exchange(blocks, ZC).reshape(8, batches, source_n, 128)
    local, own1 = heads(after(queries, blocks), keys, values, head_grad, 1, local)
    minus0, plus0, own1, own0_s, quarter = lax.optimization_barrier(
        (minus0, plus0, own1, own0_s, quarter)
    )
    weight_m, weight_p = lax.optimization_barrier((weight_m, weight_p, minus0))[:2]

    far0 = shift(minus0, "zhi", 1)
    plus1 = shift(own1, "zhi", -1)
    weight_2 = shift(after(stacked, weight_m), "x", 2)
    minus0, plus0 = lax.optimization_barrier((minus0, plus0, weight_m, weight_p))[:2]
    minus0_s, plus0_s, own1_s = swap(minus0), swap(plus0), swap(own1)
    far0, plus1, quarter, minus0_s, plus0_s = lax.optimization_barrier(
        (far0, plus1, quarter, minus0_s, plus0_s)
    )

    minus1 = shift(after(own1, far0), "zhi", 1)
    far1 = shift(plus1, "zhi", -1)
    far0_s, plus1_s = swap(far0), swap(plus1)
    quarters = [quarter] + [shift(quarter, "y", -r) for r in (1, 2, 3)]
    weights = (stacked, weight_p, weight_2, weight_m)
    blocks0 = (own0, minus0, plus0, far0, own0_s, minus0_s, plus0_s, far0_s)
    returned, plain, all0 = return_blocks(0, weights, blocks0)
    columns, flipped = gather_columns(after(quarters[0], returned), *quarters[1:])
    minus1, far1, columns, flipped = lax.optimization_barrier((minus1, far1, columns, flipped))

    minus1_s, far1_s = swap(minus1), swap(far1)
    blocks1 = (own1, minus1, plus1, far1, own1_s, minus1_s, plus1_s, far1_s)
    returned, gain_part, all1 = return_blocks(1, weights, blocks1, columns, plain, returned)
    layers = exchange(returned, SEC)
    query_in = lax.ppermute(
        after(local, minus1_s, far1_s), SEC, [(s, s - 1) for s in range(1, 8)]
    )
    gains = [gain_part] + [shift(gain_part, "x", r) for r in (1, 2, 3)]
    part = weight_blocks(after(flipped, returned), all0, all1)
    sums = sum_layers(after(layers, part[0]), gains)
    own = exchange(sums, ZC)
    own_part, sum_p, sum_m, raw_p, raw_m, far_p, far_m = part
    far_p, far_m, raw_p, raw_m = lax.optimization_barrier((far_p, far_m, raw_p, raw_m, *gains))[:4]
    far_p, far_m = shift(far_p, "x", 1), shift(far_m, "x", -1)
    raw_p, raw_m = shift(raw_p, "x", 1), shift(raw_m, "x", -1)
    far_p, far_m = lax.optimization_barrier((far_p, far_m, raw_p, raw_m))[:2]
    sum_p, sum_m = relay_blocks(sum_p, sum_m, far_p, far_m)
    packed = encoder_rows(after(own, query_in), hidden, gain)
    sum_p, sum_m = shift(sum_p, "x", 1), shift(sum_m, "x", -1)
    other = lax.ppermute(packed, "zlo", [(0, 1), (1, 0)])
    packed = jnp.stack([packed, other])
    packed = [packed] + [shift(packed, "y", -r) for r in (1, 2, 3)]
    grad_key, grad_value = add_blocks(own_part, sum_p, sum_m, raw_p, raw_m)
    query_grad = hand_on(query_in)
    encoder_grad, gain_grad = finish(packed, gain)
    return (
        query_grad,
        grad_key[None],
        grad_value[None],
        encoder_grad.reshape(pre_norm.shape),
        gain_grad.reshape(features),
    )


def solution(mesh):
    grid = Mesh(mesh.devices.reshape(4, 2, 4, 4, 2), ("y", "zlo", "zhi", "x", "core"))
    dp = ("zhi", "x", "core")
    return jax.shard_map(
        body,
        mesh=grid,
        in_specs=(
            P(None, dp, None, None),
            P(),
            P(SEC, None, dp, None, None),
            P(SEC, None, dp, None, None),
            P(SEC, None, dp, None, None),
            P(SEC, None, dp, None, None),
            P(SEC, dp, None),
            P(SEC, dp, None),
        ),
        out_specs=(
            P(SEC, None, dp, None, None),
            P(SEC, dp, None),
            P(SEC, dp, None),
            P(None, dp, None, None),
            P(),
        ),
        check_vma=False,
    )
```
